128 devices in a mesh: tm: 16 (over x_lo, y, core), height: 8 (over z, x_hi).
Axes of the slice: x: 4 (x_hi: 2, x_lo: 2; x = x_hi * 2 + x_lo), y: 4, z: 4, core: 2. Of those that a mesh axis runs over, the one named last changes fastest.
Arguments:
- queries: bfloat16 [16, 8, 1, 384, 256], P('tm', 'height'), may hold values from -24 to 24
- key_states: bfloat16 [16, 8, 1, 384, 256], P('tm', 'height'), may hold values from -24 to 24
- value_states: bfloat16 [16, 8, 1, 384, 256], P('tm', 'height'), may hold values from -6 to 6
- out_grad: bfloat16 [16, 8, 1, 384, 256], P('tm', 'height'), may hold values from -6 to 6
- clip_start: int32 [1], replicated, may hold values from 1 to 15
Outputs:
- attended: bfloat16 [16, 8, 1, 384, 256], P('tm', 'height')
- query_grad: bfloat16 [16, 8, 1, 384, 256], P('tm', 'height')
- key_grad: bfloat16 [16, 8, 1, 384, 256], P('tm', 'height')
- value_grad: bfloat16 [16, 8, 1, 384, 256], P('tm', 'height')
The draws below stay inside these ranges and needn't reach their ends.
All inputs are finite; a program needn't handle non-finite values.
Results may differ from the reference program's by a relative error of at most 0.0072.
Values may be sent and summed in bfloat16 or wider, within the bound.
A program may use at most 64 MiB of HBM per device.

```python
import jax
import jax.numpy as jnp
from jax import lax

HD = 128
HEADS = 2
TILE = 384
NW = 1
NT = 16
NH = 8


def key_base(key):
    shape = (NT, NH, NW, TILE, HEADS * HD)
    normal = jax.random.normal(key, shape, jnp.float32)
    return jnp.clip(normal, -24.0, 24.0)


def draw_key_states(key, part):
    return key_base(key).astype(jnp.bfloat16)


def draw_queries(key, part):
    own_key = jax.random.fold_in(key, 5)
    shape = (NT, NH, NW, TILE, HEADS * HD)
    normal = jnp.clip(jax.random.normal(own_key, shape, jnp.float32), -6.0, 6.0)
    values = normal
    return values.astype(jnp.bfloat16)


def steps_of(rng, dims, pieces, low, largest):
    gain, own = 1.0, jax.random.fold_in(rng, 6)
    for position, parts in pieces:
        steps = jnp.exp(jax.random.uniform(jax.random.fold_in(own, position), (parts,), jnp.float32, low / len(pieces), largest / len(pieces)))
        gain = gain * jnp.repeat(steps, dims[position] // parts).reshape([-1 if axis == position else 1 for axis in range(len(dims))])
    return gain


def noise(rng, extent, scale, reach, pieces=(), held_as=jnp.bfloat16):
    entries = scale * jax.random.normal(rng, extent, jnp.float32)
    if pieces:
        entries = entries * steps_of(rng, extent, pieces, -0.22, 0.18)
    return jnp.clip(entries, -reach, reach).astype(held_as)


def setup_inputs(seed: int = 0) -> dict:
    key_list = jax.random.split(jax.random.key(seed), 6)
    return {
        "queries": draw_queries(jax.random.fold_in(key_list[5], 71), 0),
        "key_states": draw_key_states(jax.random.fold_in(key_list[5], 71), 0),
        "value_states": noise(key_list[2], (NT, NH, NW, TILE, HEADS * HD), 1.0, 6.0, ((0, 16), (1, 8))),
        "out_grad": noise(key_list[3], (NT, NH, NW, TILE, HEADS * HD), 1.0, 6.0, ((0, 16), (1, 8))),
        "clip_start": jax.random.randint(key_list[4], (1,), 1, NT).astype(jnp.int32),
    }


NEGATIVE = -1e30


def tile_mask(time_index, row_index, clip_first, time_count, row_count, width_tiles):
    offsets = jnp.arange(3, dtype=jnp.int32) - 1
    key_time = time_index + offsets
    key_row = row_index + offsets
    time_valid = (key_time >= 0) & (key_time < time_count) & ((key_time >= clip_first) == (time_index >= clip_first))
    row_valid = (key_row >= 0) & (key_row < row_count)
    columns = jnp.arange(width_tiles, dtype=jnp.int32)
    width_valid = jnp.abs(columns[:, None] - columns[None, :]) <= 1
    combined = time_valid[:, None, None, None] & row_valid[None, :, None, None] & width_valid[None, None, :, :]
    return jnp.transpose(combined, (2, 0, 1, 3)).reshape(width_tiles, 9 * width_tiles)


def head_scores(left_rows, right_rows, validity, left_tiles, right_tiles):
    scores = jnp.dot(left_rows, right_rows.T, preferred_element_type=jnp.float32) * (left_rows.shape[1] ** -0.5)
    tile_len = left_rows.shape[0] // left_tiles
    blocked = scores.reshape(left_tiles, tile_len, right_tiles, tile_len)
    blocked = jnp.where(validity[:, None, :, None], blocked, NEGATIVE)
    return blocked.reshape(scores.shape)


def block_grads(own_queries, near_keys, near_values, own_grad, validity, width_tiles):
    scale = HD ** -0.5
    score_list, total_list, output_list = [], [], []
    for head_number in range(HEADS):
        lower = head_number * HD
        upper = lower + HD
        scores = head_scores(own_queries[:, lower:upper], near_keys[:, lower:upper], validity, width_tiles, 9 * width_tiles)
        row_max = jnp.max(scores, axis=1, keepdims=True)
        log_total = row_max + jnp.log(jnp.sum(jnp.exp(scores - row_max), axis=1, keepdims=True))
        weights = jnp.exp(scores - log_total).astype(jnp.bfloat16)
        output_list.append(jnp.dot(weights, near_values[:, lower:upper], preferred_element_type=jnp.float32))
        score_list.append(scores)
        total_list.append(log_total)
    attended = jnp.concatenate(output_list, axis=1).astype(jnp.bfloat16)
    query_parts, key_parts, value_parts = [], [], []
    for head_number in range(HEADS):
        lower = head_number * HD
        upper = lower + HD
        grad_head = own_grad[:, lower:upper]
        products = jnp.sum(grad_head.astype(jnp.float32) * attended[:, lower:upper].astype(jnp.float32), axis=1, keepdims=True)
        probability = jnp.exp(score_list[head_number] - total_list[head_number])
        weights = probability.astype(jnp.bfloat16)
        grad_weights = jnp.dot(grad_head, near_values[:, lower:upper].T, preferred_element_type=jnp.float32)
        grad_scores = (probability * (grad_weights - products)).astype(jnp.bfloat16)
        query_parts.append(jnp.dot(grad_scores, near_keys[:, lower:upper], preferred_element_type=jnp.float32) * scale)
        key_parts.append(jnp.dot(grad_scores.T, own_queries[:, lower:upper], preferred_element_type=jnp.float32) * scale)
        value_parts.append(jnp.dot(weights.T, grad_head, preferred_element_type=jnp.float32))
    query_grad = jnp.concatenate(query_parts, axis=1).astype(jnp.bfloat16)
    return attended, query_grad, jnp.concatenate(key_parts + value_parts, axis=1)


def reference(queries, key_states, value_states, out_grad, clip_start):
    clip_first = clip_start[0]
    channels = HEADS * HD
    padding = ((1, 1), (1, 1), (0, 0), (0, 0), (0, 0))
    key_pad = jnp.pad(key_states, padding)
    value_pad = jnp.pad(value_states, padding)

    def visit_block(accumulated, block_index):
        time_index = block_index // NH
        row_index = block_index % NH
        zero_index = jnp.zeros((), jnp.int32)
        corner = (time_index, row_index, zero_index, zero_index, zero_index)
        near_keys = lax.dynamic_slice(key_pad, corner, (3, 3, NW, TILE, channels)).reshape(9 * NW * TILE, channels)
        near_values = lax.dynamic_slice(value_pad, corner, (3, 3, NW, TILE, channels)).reshape(9 * NW * TILE, channels)
        own_queries = lax.dynamic_slice(queries, corner, (1, 1, NW, TILE, channels)).reshape(NW * TILE, channels)
        own_grad = lax.dynamic_slice(out_grad, corner, (1, 1, NW, TILE, channels)).reshape(NW * TILE, channels)
        validity = tile_mask(time_index, row_index, clip_first, NT, NH, NW)
        attended, query_grad, packed = block_grads(own_queries, near_keys, near_values, own_grad, validity, NW)
        previous = lax.dynamic_slice(accumulated, corner, (3, 3, NW, TILE, 2 * channels))
        accumulated = lax.dynamic_update_slice(accumulated, previous + packed.reshape(3, 3, NW, TILE, 2 * channels), corner)
        return accumulated, (attended, query_grad)

    initial = jnp.zeros((NT + 2, NH + 2, NW, TILE, 2 * channels), jnp.float32)
    accumulated, (attended, query_grad) = lax.scan(visit_block, initial, jnp.arange(NT * NH, dtype=jnp.int32))
    inner = accumulated[1:-1, 1:-1]
    shape = (NT, NH, NW, TILE, channels)
    return (attended.reshape(shape), query_grad.reshape(shape),
            inner[..., :channels].astype(jnp.bfloat16), inner[..., channels:].astype(jnp.bfloat16))
```

```python
import functools

import jax
import jax.numpy as jnp
from jax import lax
from jax.experimental import pallas as pl
from jax.experimental.pallas import tpu as pltpu
from jax.sharding import PartitionSpec as P

HEADS = 2
LOG2E = 1.4426950408889634
NEGATIVE = -1e30
MESH = pl.DeviceIdType.MESH
K, V, Q, G, STATS = range(5)


def nt(left, right):
    return lax.dot_general(left, right, (((1,), (1,)), ((), ())), preferred_element_type=jnp.float32)


def nn(left, right):
    return jnp.dot(left, right, preferred_element_type=jnp.float32)


def kernel(
    clip_ref, q_in, k_in, v_in, g_in, att_out, dq_out, dk_out, dv_out,
    tiles, stats, acc, grad, row_max, row_sum, row_dot, key_acc, value_acc,
    local_sem, swap_send, swap_recv, z_send, z_recv, tm_send, tm_recv,
):
    t = lax.axis_index("tm")
    h = lax.axis_index("height")
    core, odd, z = t % 2, h % 2, h // 2
    dim = q_in.shape[-1] // HEADS
    scale = dim ** (-0.5)
    to_log2 = scale * LOG2E

    copies = [pltpu.make_async_copy(ref, tiles.at[1, 0, u], local_sem.at[u]) for u, ref in enumerate((k_in, v_in, q_in, g_in))]
    for copy in copies:
        copy.start()

    first, last = t == 0, t == 15
    left, right = t == 7, t == 8
    relay = first | last
    two = relay | left | right
    swap_dev = (t, h + 1 - 2 * odd)
    chip_dev = (t + 1 - 2 * core, h)
    z_to = jnp.where(odd == 0, z < 3, z > 0)
    z_from = jnp.where(odd == 0, z > 0, z < 3)
    z_dst = (t, h + 2 - 4 * odd)
    z_src = (t, h - 2 + 4 * odd)
    chip_there = jnp.where(core == 0, 0, 2)
    chip_here = 2 - chip_there
    off_here = chip_there
    near = jnp.where(core == 1, t + 1, t - 1)
    near_slot = jnp.where(core == 1, 0, 2)
    off_dev = (
        jnp.where(left, 15, jnp.where(right, 0, jnp.where(last, 8, jnp.where(first, 7, near)))),
        jnp.where(left, 0, jnp.where(right, 15, jnp.where(last, 7, jnp.where(first, 8, near)))),
    )
    off_slot = (
        jnp.where(left | first, 2, jnp.where(right | last, 0, near_slot)),
        jnp.where(left | first, 0, jnp.where(right | last, 2, near_slot)),
    )
    off_from = jnp.where(last, 2, jnp.where(first, 0, 1))

    barrier = pltpu.get_barrier_semaphore()

    def greet(device):
        pl.semaphore_signal(barrier, inc=1, device_id=device, device_id_type=MESH)

    greet(swap_dev)
    greet(chip_dev)
    greet((off_dev[0], h))

    @pl.when(two)
    def _():
        greet((off_dev[1], h))

    @pl.when(z_from)
    def _():
        greet(z_src)

    pl.semaphore_wait(barrier, 3 + two.astype(jnp.int32) + z_to.astype(jnp.int32))

    def part(a, s, u):
        return stats.at[a, s] if u == STATS else tiles.at[a, s, u]

    def remote(src, dst, send, recv, device):
        return pltpu.make_async_remote_copy(
            src_ref=src, dst_ref=dst, send_sem=send, recv_sem=recv, device_id=device, device_id_type=MESH
        )

    def swap(u):
        return remote(part(1, 0, u), part(1, 1, u), swap_send.at[u], swap_recv.at[u], swap_dev)

    def along_z(u):
        return remote(part(1, 1, u), part(1, 2, u), z_send.at[u], z_recv.at[u], z_dst)

    def to_chip(s, u):
        return remote(part(1, s, u), part(chip_there, s, u), tm_send.at[0, s, u], tm_recv.at[chip_there, s, u], chip_dev)

    def off_chip(s, u):
        device, slot = off_dev[u % 2], off_slot[u % 2]
        return remote(part(off_from, s, u), part(slot, s, u), tm_send.at[1, s, u], tm_recv.at[slot, s, u], (device, h))

    def arrive(a, s, u):
        remote(part(1, s, u), part(a, s, u), tm_send.at[0, s, u], tm_recv.at[a, s, u], chip_dev).wait_recv()

    def spread(s, u):
        to_chip(s, u).start()

        @pl.when(~relay)
        def _():
            off_chip(s, u).start()

    def on_swap(u):
        swap(u).wait_recv()

        @pl.when(z_to)
        def _():
            along_z(u).start()

        spread(1, u)

    def on_z(u):
        @pl.when(z_from)
        def _():
            along_z(u).wait_recv()
            spread(2, u)

    def on_relay(s, u):
        @pl.when(relay & z_from if s == 2 else relay)
        def _():
            arrive(off_here, s, u)
            off_chip(s, u).start()

    for copy in copies:
        copy.wait()
    for u in (K, V, Q, G):
        swap(u).start()
        spread(0, u)

    clip = clip_ref[0]

    def place(i):
        s, o = i // 3, i % 3
        a = jnp.where(o == 0, 1, jnp.where(o == 1, chip_here, off_here))
        there = ((s < 2) | z_from) & ((o < 2) | ~relay)
        related = ((t + a - 1) >= clip) == (t >= clip)
        return s, o, a, there, related

    def columns(n):
        return slice(n * dim, (n + 1) * dim)

    row_max[...] = jnp.full(row_max.shape, NEGATIVE, jnp.float32)
    for ref in (acc, grad, row_sum, row_dot, key_acc, value_acc):
        ref[...] = jnp.zeros(ref.shape, ref.dtype)

    first_events = {
        1: [(on_relay, 0, K)],
        2: [(on_swap, K), (on_relay, 0, V)],
        3: [(on_swap, V), (on_relay, 0, Q)],
        4: [(on_relay, 1, K), (on_z, K), (on_relay, 0, G)],
        5: [(on_swap, Q), (on_relay, 1, V)],
        6: [(on_z, V), (on_relay, 2, K)],
        7: [(on_swap, G), (on_relay, 1, Q)],
        8: [(on_z, Q), (on_relay, 2, V), (on_relay, 1, G)],
    }
    second_events = {
        1: [(on_swap, STATS), (on_relay, 0, STATS)],
        2: [(on_z, G), (on_relay, 2, Q)],
        3: [(on_z, STATS), (on_relay, 1, STATS)],
        4: [(on_relay, 2, G), (on_relay, 2, STATS)],
    }

    def run(events, i):
        for step, entries in events.items():
            @pl.when(i == step)
            def _():
                for entry in entries:
                    entry[0](*entry[1:])

    def queries_side(i, carry):
        run(first_events, i)
        s, o, a, there, related = place(i)

        @pl.when(there & (o > 0))
        def _():
            arrive(a, s, K)
            arrive(a, s, V)

        @pl.when(there)
        def _():
            for n in range(HEADS):
                own_q, own_g = tiles[1, 0, Q, :, columns(n)], tiles[1, 0, G, :, columns(n)]
                key, value = tiles[a, s, K, :, columns(n)], tiles[a, s, V, :, columns(n)]
                scores = nt(own_q, key)
                top = jnp.where(related, jnp.max(scores, axis=1, keepdims=True) * to_log2, NEGATIVE)
                old_max = row_max[n]
                new_max = jnp.maximum(old_max, top)
                fade = jnp.exp2(old_max - new_max)
                raised = jnp.exp2(scores * to_log2 - jnp.where(related, new_max, -NEGATIVE))
                total = row_sum[n] * fade + jnp.sum(raised, axis=1, keepdims=True)
                old = acc[n]
                new = old * fade + nn(raised.astype(jnp.bfloat16), jnp.concatenate([value, key], axis=1))
                old_dot = row_dot[n]
                dot = jnp.sum(own_g.astype(jnp.float32) * new[:, :dim], axis=1, keepdims=True) / total
                inner = (raised * (nt(own_g, value) - dot)).astype(jnp.bfloat16)
                grad[n] = (grad[n] - (dot - old_dot) * old[:, dim:]) * fade + nn(inner, key)
                acc[n] = new
                row_max[n] = new_max
                row_sum[n] = total
                row_dot[n] = dot

        return carry

    lax.fori_loop(0, 9, queries_side, 0)

    lanes = lax.broadcasted_iota(jnp.int32, (q_in.shape[0], 128), 1)
    table = jnp.zeros((q_in.shape[0], 128), jnp.float32)
    finish = []
    for n in range(HEADS):
        total = row_sum[n]
        sums = acc[n]
        attended = (sums[:, :dim] / total).astype(jnp.bfloat16)
        att_out[:, columns(n)] = attended
        dot = jnp.sum(tiles[1, 0, G, :, columns(n)].astype(jnp.float32) * attended.astype(jnp.float32), axis=1, keepdims=True)
        table = jnp.where(lanes == n, row_max[n] + jnp.log2(total), table)
        table = jnp.where(lanes == HEADS + n, dot, table)
        finish.append((dot, total, sums))
    stats[1, 0] = table.T[:8]
    swap(STATS).start()
    spread(0, STATS)
    for n in range(HEADS):
        dot, total, sums = finish[n]
        dq_out[:, columns(n)] = ((grad[n] - (dot - row_dot[n]) * sums[:, dim:]) * (scale / total)).astype(jnp.bfloat16)

    def keys_side(i, carry):
        run(second_events, i)
        s, o, a, there, related = place(i)

        @pl.when(there & (o > 0))
        def _():
            arrive(a, s, Q)
            arrive(a, s, G)
            arrive(a, s, STATS)

        @pl.when(there)
        def _():
            for n in range(HEADS):
                own_k, own_v = tiles[1, 0, K, :, columns(n)], tiles[1, 0, V, :, columns(n)]
                query, out_grad = tiles[a, s, Q, :, columns(n)], tiles[a, s, G, :, columns(n)]
                log_total = jnp.where(related, stats[a, s, n : n + 1], -NEGATIVE)
                dot = stats[a, s, HEADS + n : HEADS + n + 1]
                weights = jnp.exp2(nt(own_k, query) * to_log2 - log_total)
                inner = (weights * (nt(own_v, out_grad) - dot)).astype(jnp.bfloat16)
                value_acc[n] += nn(weights.astype(jnp.bfloat16), out_grad)
                key_acc[n] += nn(inner, query)

        return carry

    lax.fori_loop(0, 9, keys_side, 0)

    for n in range(HEADS):
        dk_out[:, columns(n)] = (key_acc[n] * scale).astype(jnp.bfloat16)
        dv_out[:, columns(n)] = value_acc[n].astype(jnp.bfloat16)

    for u in (K, V, Q, G, STATS):
        swap(u).wait_send()
        for s in range(2):
            to_chip(s, u).wait_send()
            off_chip(s, u).wait_send()

        @pl.when(z_to)
        def _():
            along_z(u).wait_send()

        @pl.when(z_from)
        def _():
            to_chip(2, u).wait_send()
            off_chip(2, u).wait_send()


def shards(queries, key_states, value_states, out_grad, clip_start):
    rows, channels = queries.shape[-2:]
    dim = channels // HEADS
    flat = [x.reshape(rows, channels) for x in (queries, key_states, value_states, out_grad)]
    vmem = pl.BlockSpec(memory_space=pltpu.VMEM)
    anywhere = pl.BlockSpec(memory_space=pl.ANY)
    outs = pl.pallas_call(
        kernel,
        out_shape=[jax.ShapeDtypeStruct((rows, channels), jnp.bfloat16)] * 4,
        in_specs=[pl.BlockSpec(memory_space=pltpu.SMEM)] + [anywhere] * 4,
        out_specs=[vmem] * 4,
        scratch_shapes=[
            pltpu.VMEM((3, 3, 4, rows, channels), jnp.bfloat16),
            pltpu.VMEM((3, 3, 8, rows), jnp.float32),
            pltpu.VMEM((HEADS, rows, 2 * dim), jnp.float32),
            pltpu.VMEM((HEADS, rows, dim), jnp.float32),
            pltpu.VMEM((HEADS, rows, 1), jnp.float32),
            pltpu.VMEM((HEADS, rows, 1), jnp.float32),
            pltpu.VMEM((HEADS, rows, 1), jnp.float32),
            pltpu.VMEM((HEADS, rows, dim), jnp.float32),
            pltpu.VMEM((HEADS, rows, dim), jnp.float32),
            pltpu.SemaphoreType.DMA((4,)),
            pltpu.SemaphoreType.DMA((5,)),
            pltpu.SemaphoreType.DMA((5,)),
            pltpu.SemaphoreType.DMA((5,)),
            pltpu.SemaphoreType.DMA((5,)),
            pltpu.SemaphoreType.DMA((2, 3, 5)),
            pltpu.SemaphoreType.DMA((3, 3, 5)),
        ],
        compiler_params=pltpu.CompilerParams(
            collective_id=0, has_side_effects=True, vmem_limit_bytes=48 * 2**20
        ),
        name="tile_attention",
    )(clip_start, *flat)
    return tuple(x.reshape(queries.shape) for x in outs)


def solution(mesh):
    spec = P("tm", "height", None, None, None)
    return jax.shard_map(
        shards, mesh=mesh, in_specs=(spec,) * 4 + (P(),), out_specs=(spec,) * 4, check_vma=False
    )
```

```python
import functools

import jax
import jax.numpy as jnp
from jax import lax
from jax.experimental import pallas as pl
from jax.experimental.pallas import tpu as pltpu
from jax.sharding import PartitionSpec as P

HEADS = 2
LOG2E = 1.4426950408889634
NEGATIVE = -1e30
MESH = pl.DeviceIdType.MESH
K, V, Q, G, STATS = range(5)


def nt(left, right):
    return lax.dot_general(left, right, (((1,), (1,)), ((), ())), preferred_element_type=jnp.float32)


def nn(left, right):
    return jnp.dot(left, right, preferred_element_type=jnp.float32)


def kernel(
    clip_ref, q_in, k_in, v_in, g_in, att_out, dq_out, dk_out, dv_out,
    tiles, stats, out_grad_t, acc, grad, row_max, row_sum, row_dot, key_acc, value_acc,
    local_sem, swap_send, swap_recv, z_send, z_recv, tm_send, tm_recv,
):
    t = lax.axis_index("tm")
    h = lax.axis_index("height")
    core, odd, z = t % 2, h % 2, h // 2
    dim = q_in.shape[-1] // HEADS
    scale = dim ** (-0.5)
    to_log2 = scale * LOG2E

    copies = [pltpu.make_async_copy(ref, tiles.at[1, 0, u], local_sem.at[u]) for u, ref in enumerate((k_in, v_in, q_in, g_in))]
    for copy in copies:
        copy.start()

    first, last = t == 0, t == 15
    left, right = t == 7, t == 8
    relay = first | last
    two = relay | left | right
    swap_dev = (t, h + 1 - 2 * odd)
    chip_dev = (t + 1 - 2 * core, h)
    z_to = jnp.where(odd == 0, z < 3, z > 0)
    z_from = jnp.where(odd == 0, z > 0, z < 3)
    z_dst = (t, h + 2 - 4 * odd)
    z_src = (t, h - 2 + 4 * odd)
    chip_there = jnp.where(core == 0, 0, 2)
    chip_here = 2 - chip_there
    off_here = chip_there
    near = jnp.where(core == 1, t + 1, t - 1)
    near_slot = jnp.where(core == 1, 0, 2)
    off_dev = (
        jnp.where(left, 15, jnp.where(right, 0, jnp.where(last, 8, jnp.where(first, 7, near)))),
        jnp.where(left, 0, jnp.where(right, 15, jnp.where(last, 7, jnp.where(first, 8, near)))),
    )
    off_slot = (
        jnp.where(left | first, 2, jnp.where(right | last, 0, near_slot)),
        jnp.where(left | first, 0, jnp.where(right | last, 2, near_slot)),
    )
    off_from = jnp.where(last, 2, jnp.where(first, 0, 1))

    barrier = pltpu.get_barrier_semaphore()

    def greet(device):
        pl.semaphore_signal(barrier, inc=1, device_id=device, device_id_type=MESH)

    greet(swap_dev)
    greet(chip_dev)
    greet((off_dev[0], h))

    @pl.when(two)
    def _():
        greet((off_dev[1], h))

    @pl.when(z_from)
    def _():
        greet(z_src)

    pl.semaphore_wait(barrier, 3 + two.astype(jnp.int32) + z_to.astype(jnp.int32))

    def part(a, s, u):
        return stats.at[a, s] if u == STATS else tiles.at[a, s, u]

    def remote(src, dst, send, recv, device):
        return pltpu.make_async_remote_copy(
            src_ref=src, dst_ref=dst, send_sem=send, recv_sem=recv, device_id=device, device_id_type=MESH
        )

    def swap(u):
        return remote(part(1, 0, u), part(1, 1, u), swap_send.at[u], swap_recv.at[u], swap_dev)

    def along_z(u):
        return remote(part(1, 1, u), part(1, 2, u), z_send.at[u], z_recv.at[u], z_dst)

    def to_chip(s, u):
        return remote(part(1, s, u), part(chip_there, s, u), tm_send.at[0, s, u], tm_recv.at[chip_there, s, u], chip_dev)

    def off_chip(s, u):
        device, slot = off_dev[u % 2], off_slot[u % 2]
        return remote(part(off_from, s, u), part(slot, s, u), tm_send.at[1, s, u], tm_recv.at[slot, s, u], (device, h))

    def arrive(a, s, u):
        remote(part(1, s, u), part(a, s, u), tm_send.at[0, s, u], tm_recv.at[a, s, u], chip_dev).wait_recv()

    def spread(s, u):
        to_chip(s, u).start()

        @pl.when(~relay)
        def _():
            off_chip(s, u).start()

    def on_swap(u):
        swap(u).wait_recv()

        @pl.when(z_to)
        def _():
            along_z(u).start()

        spread(1, u)

    def on_z(u):
        @pl.when(z_from)
        def _():
            along_z(u).wait_recv()
            spread(2, u)

    def on_relay(s, u):
        @pl.when(relay & z_from if s == 2 else relay)
        def _():
            arrive(off_here, s, u)
            off_chip(s, u).start()

    for copy in copies:
        copy.wait()
    for u in (K, V, Q, G):
        swap(u).start()
        spread(0, u)

    clip = clip_ref[0]

    def place(i):
        s, o = i // 3, i % 3
        a = jnp.where(o == 0, 1, jnp.where(o == 1, chip_here, off_here))
        there = ((s < 2) | z_from) & ((o < 2) | ~relay)
        related = ((t + a - 1) >= clip) == (t >= clip)
        return s, o, a, there, related

    def columns(n):
        return slice(n * dim, (n + 1) * dim)

    row_max[...] = jnp.full(row_max.shape, NEGATIVE, jnp.float32)
    for ref in (acc, grad, row_sum, row_dot, key_acc, value_acc):
        ref[...] = jnp.zeros(ref.shape, ref.dtype)
    stats[1, 0] = jnp.zeros(stats.shape[2:], jnp.float32)
    for n in range(HEADS):
        out_grad_t[n] = tiles[1, 0, G, :, columns(n)].astype(jnp.float32).T

    first_events = {
        1: [(on_relay, 0, K)],
        2: [(on_swap, K), (on_relay, 0, V)],
        3: [(on_swap, V), (on_relay, 0, Q)],
        4: [(on_relay, 1, K), (on_z, K), (on_relay, 0, G)],
        5: [(on_swap, Q), (on_relay, 1, V)],
        6: [(on_z, V), (on_relay, 2, K)],
        7: [(on_swap, G), (on_relay, 1, Q)],
        8: [(on_z, Q), (on_relay, 2, V), (on_relay, 1, G)],
    }
    second_events = {
        1: [(on_swap, STATS), (on_relay, 0, STATS)],
        2: [(on_z, G), (on_relay, 2, Q)],
        3: [(on_z, STATS), (on_relay, 1, STATS)],
        4: [(on_relay, 2, G), (on_relay, 2, STATS)],
    }

    def run(events, i):
        for step, entries in events.items():
            @pl.when(i == step)
            def _():
                for entry in entries:
                    entry[0](*entry[1:])

    def queries_side(i, carry):
        run(first_events, i)
        s, o, a, there, related = place(i)

        @pl.when(there & (o > 0))
        def _():
            arrive(a, s, K)
            arrive(a, s, V)

        @pl.when(there)
        def _():
            heads = range(HEADS)
            key = [tiles[a, s, K, :, columns(n)] for n in heads]
            value = [tiles[a, s, V, :, columns(n)] for n in heads]
            scores = [nt(key[n], tiles[1, 0, Q, :, columns(n)]) for n in heads]
            grad_weights = [nt(value[n], tiles[1, 0, G, :, columns(n)]) for n in heads]
            key_t = [key[n].T for n in heads]
            both_t = [jnp.concatenate([value[n].T, key_t[n]], axis=0) for n in heads]
            fades, raised, totals, dots = [], [], [], []
            for n in heads:
                top = jnp.where(related, jnp.max(scores[n], axis=0, keepdims=True) * to_log2, NEGATIVE)
                old_max = row_max[n]
                new_max = jnp.maximum(old_max, top)
                fades.append(jnp.exp2(old_max - new_max))
                raised.append(jnp.exp2(scores[n] * to_log2 - jnp.where(related, new_max, -NEGATIVE)))
                totals.append(row_sum[n] * fades[n] + jnp.sum(raised[n], axis=0, keepdims=True))
                row_max[n] = new_max
                row_sum[n] = totals[n]
            for n in heads:
                old = acc[n]
                new = old * fades[n] + nn(both_t[n], raised[n].astype(jnp.bfloat16))
                dots.append(jnp.sum(out_grad_t[n] * new[:dim], axis=0, keepdims=True) / totals[n])
                grad[n] = (grad[n] - (dots[n] - row_dot[n]) * old[dim:]) * fades[n]
                acc[n] = new
                row_dot[n] = dots[n]
            for n in heads:
                inner = (raised[n] * (grad_weights[n] - dots[n])).astype(jnp.bfloat16)
                grad[n] += nn(key_t[n], inner)

        return carry

    lax.fori_loop(0, 9, queries_side, 0)

    finish = []
    for n in range(HEADS):
        total = row_sum[n]
        sums = acc[n]
        attended = (sums[:dim] / total).astype(jnp.bfloat16).astype(jnp.float32)
        dot = jnp.sum(out_grad_t[n] * attended, axis=0, keepdims=True)
        stats[1, 0, n : n + 1] = row_max[n] + jnp.log2(total)
        stats[1, 0, HEADS + n : HEADS + n + 1] = dot
        finish.append((dot, total, sums, attended))
    swap(STATS).start()
    spread(0, STATS)
    for n in range(HEADS):
        dot, total, sums, attended = finish[n]
        att_out[:, columns(n)] = attended.T.astype(jnp.bfloat16)
        own_grad = (grad[n] - (dot - row_dot[n]) * sums[dim:]) * (scale / total)
        dq_out[:, columns(n)] = own_grad.T.astype(jnp.bfloat16)

    def keys_side(i, carry):
        run(second_events, i)
        s, o, a, there, related = place(i)

        @pl.when(there & (o > 0))
        def _():
            arrive(a, s, Q)
            arrive(a, s, G)
            arrive(a, s, STATS)

        @pl.when(there)
        def _():
            for n in range(HEADS):
                own_k, own_v = tiles[1, 0, K, :, columns(n)], tiles[1, 0, V, :, columns(n)]
                query, out_grad = tiles[a, s, Q, :, columns(n)], tiles[a, s, G, :, columns(n)]
                log_total = jnp.where(related, stats[a, s, n : n + 1], -NEGATIVE)
                dot = stats[a, s, HEADS + n : HEADS + n + 1]
                weights = jnp.exp2(nt(own_k, query) * to_log2 - log_total)
                inner = (weights * (nt(own_v, out_grad) - dot)).astype(jnp.bfloat16)
                value_acc[n] += nn(weights.astype(jnp.bfloat16), out_grad)
                key_acc[n] += nn(inner, query)

        return carry

    lax.fori_loop(0, 9, keys_side, 0)

    for n in range(HEADS):
        dk_out[:, columns(n)] = (key_acc[n] * scale).astype(jnp.bfloat16)
        dv_out[:, columns(n)] = value_acc[n].astype(jnp.bfloat16)

    for u in (K, V, Q, G, STATS):
        swap(u).wait_send()
        for s in range(2):
            to_chip(s, u).wait_send()
            off_chip(s, u).wait_send()

        @pl.when(z_to)
        def _():
            along_z(u).wait_send()

        @pl.when(z_from)
        def _():
            to_chip(2, u).wait_send()
            off_chip(2, u).wait_send()


def write_out(*refs):
    sources, targets, sems = refs[:4], refs[4:8], refs[8]
    copies = [pltpu.make_async_copy(sources[i], targets[i], sems.at[i]) for i in range(4)]
    for copy in copies:
        copy.start()
    for copy in copies:
        copy.wait()


def shards(queries, key_states, value_states, out_grad, clip_start):
    rows, channels = queries.shape[-2:]
    dim = channels // HEADS
    flat = [x.reshape(rows, channels) for x in (queries, key_states, value_states, out_grad)]
    vmem = pl.BlockSpec(memory_space=pltpu.VMEM)
    anywhere = pl.BlockSpec(memory_space=pl.ANY)
    outs = pl.pallas_call(
        kernel,
        out_shape=[jax.ShapeDtypeStruct((rows, channels), jnp.bfloat16)] * 4,
        in_specs=[pl.BlockSpec(memory_space=pltpu.SMEM)] + [pl.BlockSpec(memory_space=pltpu.HBM)] * 4,
        out_specs=[vmem] * 4,
        scratch_shapes=[
            pltpu.VMEM((3, 3, 4, rows, channels), jnp.bfloat16),
            pltpu.VMEM((3, 3, 8, rows), jnp.float32),
            pltpu.VMEM((HEADS, dim, rows), jnp.float32),
            pltpu.VMEM((HEADS, 2 * dim, rows), jnp.float32),
            pltpu.VMEM((HEADS, dim, rows), jnp.float32),
            pltpu.VMEM((HEADS, 1, rows), jnp.float32),
            pltpu.VMEM((HEADS, 1, rows), jnp.float32),
            pltpu.VMEM((HEADS, 1, rows), jnp.float32),
            pltpu.VMEM((HEADS, rows, dim), jnp.float32),
            pltpu.VMEM((HEADS, rows, dim), jnp.float32),
            pltpu.SemaphoreType.DMA((4,)),
            pltpu.SemaphoreType.DMA((5,)),
            pltpu.SemaphoreType.DMA((5,)),
            pltpu.SemaphoreType.DMA((5,)),
            pltpu.SemaphoreType.DMA((5,)),
            pltpu.SemaphoreType.DMA((2, 3, 5)),
            pltpu.SemaphoreType.DMA((3, 3, 5)),
        ],
        compiler_params=pltpu.CompilerParams(
            collective_id=0, has_side_effects=True, vmem_limit_bytes=48 * 2**20
        ),
        name="tile_attention",
    )(clip_start, *flat)
    outs = pl.pallas_call(
        write_out,
        out_shape=[jax.ShapeDtypeStruct((rows, channels), jnp.bfloat16)] * 4,
        in_specs=[anywhere] * 4,
        out_specs=[anywhere] * 4,
        scratch_shapes=[pltpu.SemaphoreType.DMA((4,))],
        name="write_out",
    )(*outs)
    return tuple(x.reshape(queries.shape) for x in outs)


def solution(mesh):
    spec = P("tm", "height", None, None, None)
    return jax.shard_map(
        shards, mesh=mesh, in_specs=(spec,) * 4 + (P(),), out_specs=(spec,) * 4, check_vma=False
    )
```

```python
import jax
import jax.numpy as jnp
from jax import lax
from jax.experimental import pallas as pl
from jax.experimental.pallas import tpu as pltpu
from jax.sharding import PartitionSpec as P

HEADS = 2
LOG2E = 1.4426950408889634
NEGATIVE = -1e30
MESH = pl.DeviceIdType.MESH
QUERIES, FINISH, KEYS, NOTHING = range(4)
K, V, Q, G = range(4)
PIECES = 2
EARLY = 2 * PIECES
CHUNKS = 4 * PIECES


def nt(left, right):
    return lax.dot_general(left, right, (((1,), (1,)), ((), ())), preferred_element_type=jnp.float32)


def nn(left, right):
    return jnp.dot(left, right, preferred_element_type=jnp.float32)


def kernel(
    clip_ref, q_in, k_in, v_in, g_in, out_ref,
    tiles, stats, out_grad_t, acc, grad, row_max, row_sum, row_dot, key_acc, value_acc,
    local_sem, swap_send, swap_recv, z_send, z_recv, tm_send, tm_recv, side_send, stats_send, stats_recv,
):
    t = lax.axis_index("tm")
    h = lax.axis_index("height")
    core, odd, z = t % 2, h % 2, h // 2
    dim = q_in.shape[-1] // HEADS
    scale = dim ** (-0.5)
    to_log2 = scale * LOG2E

    copies = [pltpu.make_async_copy(ref, tiles.at[1, 0, u], local_sem.at[u]) for u, ref in enumerate((k_in, v_in, q_in, g_in))]
    for copy in copies:
        copy.start()

    first, last, left, right = t == 0, t == 15, t == 7, t == 8
    relay, bound = first | last, left | right
    other = h + 1 - 2 * odd
    chip_dev = (t + 1 - 2 * core, h)
    z_to = jnp.where(odd == 0, z < 3, z > 0)
    z_from = jnp.where(odd == 0, z > 0, z < 3)
    z_dst = (t, h + 2 - 4 * odd)
    z_src = (t, h - 2 + 4 * odd)
    chip_there = jnp.where(core == 0, 0, 2)
    chip_here = 2 - chip_there
    off_here = chip_there
    near = jnp.where(core == 1, t + 1, t - 1)
    near_slot = jnp.where(core == 1, 0, 2)

    def pick(at_left, at_right, at_last, at_first, usual):
        return jnp.where(left, at_left, jnp.where(right, at_right, jnp.where(last, at_last, jnp.where(first, at_first, usual))))

    own_dev, own_slot = pick(0, 15, 7, 8, near), pick(0, 2, 2, 0, near_slot)
    off_from = pick(1, 1, 2, 0, 1)

    neighbours = [(dt, dh) for dt in (-1, 0, 1) for dh in (-1, 0, 1) if dt or dh]

    def exists(dt, dh):
        return (t + dt >= 0) & (t + dt <= 15) & (h + dh >= 0) & (h + dh <= 7)

    barrier = pltpu.get_barrier_semaphore()

    def greet(frame, row):
        pl.semaphore_signal(barrier, inc=1, device_id=(frame, row), device_id_type=MESH)

    targets = (relay | bound).astype(jnp.int32) + z_to.astype(jnp.int32)
    for dt, dh in neighbours:
        targets = targets + exists(dt, dh).astype(jnp.int32)

        @pl.when(exists(dt, dh))
        def _():
            greet(t + dt, h + dh)

    @pl.when(relay | bound)
    def _():
        greet(pick(15, 0, 8, 7, 0), h)

    @pl.when(z_from)
    def _():
        greet(*z_src)

    pl.semaphore_wait(barrier, targets)

    def part(a, s, k):
        u, piece = k // PIECES, k % PIECES
        size = tiles.shape[3] // PIECES
        return tiles.at[a, s, u, pl.ds(piece * size, size)]

    def remote(src, dst, send, recv, device):
        return pltpu.make_async_remote_copy(
            src_ref=src, dst_ref=dst, send_sem=send, recv_sem=recv, device_id=device, device_id_type=MESH
        )

    def swap(k):
        return remote(part(1, 0, k), part(1, 1, k), swap_send.at[k], swap_recv.at[k], (t, other))

    def along_z(k):
        return remote(part(1, 1, k), part(1, 2, k), z_send.at[k], z_recv.at[k], z_dst)

    def side_z(k):
        return remote(part(off_here, 1, k), part(off_here, 2, k), side_send.at[k], tm_recv.at[off_here, 2, k], z_dst)

    def to_chip(s, k):
        return remote(part(1, s, k), part(chip_there, s, k), tm_send.at[0, s, k], tm_recv.at[chip_there, s, k], chip_dev)

    def off_chip(s, k):
        frame, slot = (near, near_slot) if s else (own_dev, own_slot)
        return remote(part(off_from, s, k), part(slot, s, k), tm_send.at[1, s, k], tm_recv.at[slot, s, k], (frame, h))

    def arrive(a, s, k):
        remote(part(1, s, k), part(a, s, k), tm_send.at[0, s, k], tm_recv.at[a, s, k], chip_dev).wait_recv()

    def row_stats(dt, dh):
        a = 1 - dt
        s = jnp.where(odd == (dh + 1) // 2, 2, 1) * dh * dh
        return remote(stats.at[1, 0], stats.at[a, s], stats_send.at[a, dh + 1], stats_recv.at[a, s], (t + dt, h + dh))

    def spread(s, k):
        @pl.when(~(relay | bound) if s == 2 else ~relay)
        def _():
            off_chip(s, k).start()

        to_chip(s, k).start()

    def begin(k):
        swap(k).start()
        spread(0, k)

    def on_swap(k):
        swap(k).wait_recv()

        @pl.when(z_to)
        def _():
            along_z(k).start()

        spread(1, k)

    def on_z(k):
        @pl.when(z_from)
        def _():
            along_z(k).wait_recv()
            spread(2, k)

    def on_relay(k):
        arrive(off_here, 0, k)
        off_chip(0, k).start()

    def on_side(k):
        arrive(off_here, 1, k)

        @pl.when(z_to)
        def _():
            side_z(k).start()

    for copy in copies:
        copy.wait()
    for k in range(4):
        begin(k)

    clip = clip_ref[0]

    def columns(n):
        return slice(n * dim, (n + 1) * dim)

    row_max[...] = jnp.full(row_max.shape, NEGATIVE, jnp.float32)
    for ref in (acc, grad, row_sum, row_dot, key_acc, value_acc):
        ref[...] = jnp.zeros(ref.shape, ref.dtype)
    stats[1, 0] = jnp.zeros(stats.shape[2:], jnp.float32)
    for n in range(HEADS):
        out_grad_t[n] = tiles[1, 0, G, :, columns(n)].astype(jnp.float32).T

    EVENTS = (
        {
            2: [(on_swap, 0)],
            3: [(on_swap, 1), (on_z, 0), (on_swap, 2), (on_swap, 3)],
            4: [(begin, 4), (begin, 5), (on_z, 1)],
            5: [(on_z, 2)],
            6: [(on_z, 3)],
            7: [(begin, 6), (begin, 7), (on_swap, 4)],
            8: [(on_swap, 5)],
            9: [(on_z, 4), (on_swap, 6)],
            10: [(on_z, 5), (on_swap, 7)],
            12: [(on_z, 6)],
            16: [(on_z, 7)],
        },
        {
            2: [(on_swap, 0), (on_swap, 1), (on_z, 0), (on_swap, 2), (on_z, 1), (on_swap, 3)],
            3: [(begin, 4), (begin, 5), (on_side, 0)],
            4: [(on_side, 1), (on_z, 2), (on_side, 2)],
            5: [(on_z, 3), (begin, 6), (begin, 7), (on_side, 3)],
            6: [(on_swap, 4)],
            7: [(on_swap, 5)],
            9: [(on_swap, 6)],
            10: [(on_z, 4), (on_swap, 7), (on_z, 5)],
            11: [(on_side, 4)],
            12: [(on_side, 5), (on_z, 6)],
            13: [(on_side, 6), (on_z, 7)],
            14: [(on_side, 7)],
        },
        {
            2: [(on_relay, 0), (on_relay, 1), (on_swap, 0), (on_relay, 2), (on_relay, 3), (on_swap, 1), (on_z, 0), (on_swap, 2), (on_z, 1), (on_swap, 3), (begin, 4), (begin, 5)],
            4: [(on_z, 2), (on_relay, 4), (on_z, 3)],
            5: [(begin, 6), (begin, 7), (on_relay, 5)],
            6: [(on_swap, 4)],
            7: [(on_swap, 5)],
            8: [(on_relay, 6), (on_relay, 7), (on_z, 4), (on_z, 5), (on_swap, 6)],
            9: [(on_swap, 7)],
            10: [(on_z, 6)],
            11: [(on_z, 7)],
        },
    )
    KIND = (
        (0, 0, 0, 0, 0, 0, 0, 0, 0, 1, 2, 2, 2, 2, 2, 2, 2, 2, 2, 3),
        (0, 0, 0, 0, 0, 0, 0, 0, 0, 1, 2, 2, 2, 2, 2, 2, 2, 2, 2, 3),
        (0, 0, 0, 0, 0, 0, 1, 2, 2, 2, 2, 2, 2, 3, 3, 3, 3, 3, 3, 3),
    )
    ROW = (
        (0, 0, 0, 1, 1, 1, 2, 2, 2, 0, 0, 0, 0, 1, 1, 1, 2, 2, 2, 0),
        (0, 0, 1, 1, 0, 2, 2, 1, 2, 0, 0, 0, 1, 0, 1, 2, 2, 1, 2, 0),
        (0, 0, 1, 1, 2, 2, 0, 0, 0, 1, 1, 2, 2, 0, 0, 0, 0, 0, 0, 0),
    )
    FRAME = (
        (0, 1, 2, 0, 1, 2, 0, 1, 2, 0, 0, 1, 2, 0, 1, 2, 0, 1, 2, 0),
        (0, 1, 0, 1, 2, 0, 1, 2, 2, 0, 0, 1, 0, 2, 1, 0, 1, 2, 2, 0),
        (0, 1, 0, 1, 0, 1, 0, 0, 1, 0, 1, 0, 1, 0, 0, 0, 0, 0, 0, 0),
    )
    STEPS = 20

    def choose(step, tables):
        def at(table):
            value = jnp.int32(table[-1])
            for i in range(len(table) - 2, -1, -1):
                value = jnp.where(step == i, table[i], value)
            return value

        return jnp.where(relay, at(tables[2]), jnp.where(bound, at(tables[1]), at(tables[0])))

    def queries_side(a, s, related):
        heads = range(HEADS)
        key = [tiles[a, s, K, :, columns(n)] for n in heads]
        value = [tiles[a, s, V, :, columns(n)] for n in heads]
        scores = [nt(key[n], tiles[1, 0, Q, :, columns(n)]) for n in heads]
        grad_weights = [nt(value[n], tiles[1, 0, G, :, columns(n)]) for n in heads]
        key_t = [key[n].T for n in heads]
        both_t = [jnp.concatenate([value[n].T, key_t[n]], axis=0) for n in heads]
        fades, raised, totals, dots = [], [], [], []
        for n in heads:
            top = jnp.where(related, jnp.max(scores[n], axis=0, keepdims=True) * to_log2, NEGATIVE)
            old_max = row_max[n]
            new_max = jnp.maximum(old_max, top)
            fades.append(jnp.exp2(old_max - new_max))
            raised.append(jnp.exp2(scores[n] * to_log2 - jnp.where(related, new_max, -NEGATIVE)))
            totals.append(row_sum[n] * fades[n] + jnp.sum(raised[n], axis=0, keepdims=True))
            row_max[n] = new_max
            row_sum[n] = totals[n]
        for n in heads:
            old = acc[n]
            new = old * fades[n] + nn(both_t[n], raised[n].astype(jnp.bfloat16))
            dots.append(jnp.sum(out_grad_t[n] * new[:dim], axis=0, keepdims=True) / totals[n])
            grad[n] = (grad[n] - (dots[n] - row_dot[n]) * old[dim:]) * fades[n]
            acc[n] = new
            row_dot[n] = dots[n]
        for n in heads:
            inner = (raised[n] * (grad_weights[n] - dots[n])).astype(jnp.bfloat16)
            grad[n] += nn(key_t[n], inner)

    def finish_queries():
        finish = []
        for n in range(HEADS):
            total = row_sum[n]
            sums = acc[n]
            attended = (sums[:dim] / total).astype(jnp.bfloat16).astype(jnp.float32)
            dot = jnp.sum(out_grad_t[n] * attended, axis=0, keepdims=True)
            stats[1, 0, n : n + 1] = row_max[n] + jnp.log2(total)
            stats[1, 0, HEADS + n : HEADS + n + 1] = dot
            finish.append((dot, total, sums, attended))
        for dt, dh in neighbours:
            @pl.when(exists(dt, dh))
            def _():
                row_stats(dt, dh).start()

        for n in range(HEADS):
            dot, total, sums, attended = finish[n]
            out_ref[0, :, columns(n)] = attended.T.astype(jnp.bfloat16)
            own_grad = (grad[n] - (dot - row_dot[n]) * sums[dim:]) * (scale / total)
            out_ref[1, :, columns(n)] = own_grad.T.astype(jnp.bfloat16)

    def keys_side(a, s, related):
        for n in range(HEADS):
            own_k, own_v = tiles[1, 0, K, :, columns(n)], tiles[1, 0, V, :, columns(n)]
            query, out_grad = tiles[a, s, Q, :, columns(n)], tiles[a, s, G, :, columns(n)]
            log_total = jnp.where(related, stats[a, s, n : n + 1], -NEGATIVE)
            dot = stats[a, s, HEADS + n : HEADS + n + 1]
            weights = jnp.exp2(nt(own_k, query) * to_log2 - log_total)
            inner = (weights * (nt(own_v, out_grad) - dot)).astype(jnp.bfloat16)
            value_acc[n] += nn(weights.astype(jnp.bfloat16), out_grad)
            key_acc[n] += nn(inner, query)

    def do_step(step, carry):
        for mine, events in zip((~(relay | bound), bound, relay), EVENTS):
            for at, entries in events.items():
                @pl.when(mine & (step == at))
                def _():
                    for entry in entries:
                        entry[0](*entry[1:])

        kind, s, o = choose(step, KIND), choose(step, ROW), choose(step, FRAME)
        a = jnp.where(o == 0, 1, jnp.where(o == 1, chip_here, off_here))
        there = ((s < 2) | z_from) & ((o < 2) | ~relay)
        related = ((t + a - 1) >= clip) == (t >= clip)
        waits = (o > 0) & ~(bound & (o == 2) & (s == 1))

        @pl.when(there & (kind == QUERIES))
        def _():
            @pl.when(waits)
            def _():
                for k in range(EARLY):
                    arrive(a, s, k)

            queries_side(a, s, related)

        @pl.when(kind == FINISH)
        def _():
            finish_queries()

        @pl.when(there & (kind == KEYS))
        def _():
            @pl.when(waits)
            def _():
                for k in range(EARLY, CHUNKS):
                    arrive(a, s, k)

            @pl.when((s > 0) | (o > 0))
            def _():
                remote(stats.at[1, 0], stats.at[a, s], stats_send.at[1, 1], stats_recv.at[a, s], chip_dev).wait_recv()

            keys_side(a, s, related)

        return carry

    lax.fori_loop(0, STEPS, do_step, 0)

    for n in range(HEADS):
        out_ref[2, :, columns(n)] = (key_acc[n] * scale).astype(jnp.bfloat16)
        out_ref[3, :, columns(n)] = value_acc[n].astype(jnp.bfloat16)

    for k in range(CHUNKS):
        to_chip(0, k).wait_send()
        off_chip(0, k).wait_send()
        to_chip(1, k).wait_send()

        @pl.when(~relay)
        def _():
            off_chip(1, k).wait_send()

        swap(k).wait_send()

        @pl.when(z_to)
        def _():
            along_z(k).wait_send()

        @pl.when(z_to & bound)
        def _():
            side_z(k).wait_send()

        @pl.when(z_from)
        def _():
            to_chip(2, k).wait_send()

        @pl.when(z_from & ~(relay | bound))
        def _():
            off_chip(2, k).wait_send()

    for dt, dh in neighbours:
        @pl.when(exists(dt, dh))
        def _():
            row_stats(dt, dh).wait_send()


def shards(queries, key_states, value_states, out_grad, clip_start):
    rows, channels = queries.shape[-2:]
    dim = channels // HEADS
    flat = [x.reshape(rows, channels) for x in (queries, key_states, value_states, out_grad)]
    vmem = pl.BlockSpec(memory_space=pltpu.VMEM)
    outs = pl.pallas_call(
        kernel,
        out_shape=jax.ShapeDtypeStruct((4, rows, channels), jnp.bfloat16),
        in_specs=[pl.BlockSpec(memory_space=pltpu.SMEM)] + [pl.BlockSpec(memory_space=pltpu.HBM)] * 4,
        out_specs=vmem,
        scratch_shapes=[
            pltpu.VMEM((3, 3, 4, rows, channels), jnp.bfloat16),
            pltpu.VMEM((3, 3, 8, rows), jnp.float32),
            pltpu.VMEM((HEADS, dim, rows), jnp.float32),
            pltpu.VMEM((HEADS, 2 * dim, rows), jnp.float32),
            pltpu.VMEM((HEADS, dim, rows), jnp.float32),
            pltpu.VMEM((HEADS, 1, rows), jnp.float32),
            pltpu.VMEM((HEADS, 1, rows), jnp.float32),
            pltpu.VMEM((HEADS, 1, rows), jnp.float32),
            pltpu.VMEM((HEADS, rows, dim), jnp.float32),
            pltpu.VMEM((HEADS, rows, dim), jnp.float32),
            pltpu.SemaphoreType.DMA((4,)),
            pltpu.SemaphoreType.DMA((CHUNKS,)),
            pltpu.SemaphoreType.DMA((CHUNKS,)),
            pltpu.SemaphoreType.DMA((CHUNKS,)),
            pltpu.SemaphoreType.DMA((CHUNKS,)),
            pltpu.SemaphoreType.DMA((2, 3, CHUNKS)),
            pltpu.SemaphoreType.DMA((3, 3, CHUNKS)),
            pltpu.SemaphoreType.DMA((CHUNKS,)),
            pltpu.SemaphoreType.DMA((3, 3)),
            pltpu.SemaphoreType.DMA((3, 3)),
        ],
        compiler_params=pltpu.CompilerParams(
            collective_id=0, has_side_effects=True, vmem_limit_bytes=64 * 2**20
        ),
        name="tile_attention",
    )(clip_start, *flat)
    return tuple(outs[i].reshape(queries.shape) for i in range(4))


def solution(mesh):
    spec = P("tm", "height", None, None, None)
    return jax.shard_map(
        shards, mesh=mesh, in_specs=(spec,) * 4 + (P(),), out_specs=(spec,) * 4, check_vma=False
    )
```

```python
import jax
import jax.numpy as jnp
from jax import lax
from jax.experimental import pallas as pl
from jax.experimental.pallas import tpu as pltpu
from jax.sharding import PartitionSpec as P

HEADS = 2
LOG2E = 1.4426950408889634
NEGATIVE = -1e30
MESH = pl.DeviceIdType.MESH
QUERIES, FINISH, KEYS, NOTHING = range(4)
K, V, Q, G = range(4)
PIECES = 2
EARLY = 2 * PIECES
CHUNKS = 4 * PIECES


def nt(left, right):
    return lax.dot_general(left, right, (((1,), (1,)), ((), ())), preferred_element_type=jnp.float32)


def nn(left, right):
    return jnp.dot(left, right, preferred_element_type=jnp.float32)


def kernel(
    clip_ref, q_in, k_in, v_in, g_in, out_ref,
    tiles, stats, out_grad_t, acc, grad, row_max, row_sum, row_dot, key_acc, value_acc,
    local_sem, sent, swap_recv, z_recv, chip_recv, off_recv, stats_send, stats_recv,
):
    t = lax.axis_index("tm")
    h = lax.axis_index("height")
    core, odd, z = t % 2, h % 2, h // 2
    dim = q_in.shape[-1] // HEADS
    scale = dim ** (-0.5)
    to_log2 = scale * LOG2E

    copies = [pltpu.make_async_copy(ref, tiles.at[1, 0, u], local_sem.at[u]) for u, ref in enumerate((k_in, v_in, q_in, g_in))]
    for copy in copies:
        copy.start()

    first, last, left, right = t == 0, t == 15, t == 7, t == 8
    relay, bound = first | last, left | right
    other = h + 1 - 2 * odd
    chip_dev = (t + 1 - 2 * core, h)
    z_to = jnp.where(odd == 0, z < 3, z > 0)
    z_from = jnp.where(odd == 0, z > 0, z < 3)
    z_dst = (t, h + 2 - 4 * odd)
    z_src = (t, h - 2 + 4 * odd)
    chip_there = jnp.where(core == 0, 0, 2)
    chip_here = 2 - chip_there
    off_here = chip_there
    near = jnp.where(core == 1, t + 1, t - 1)
    near_slot = jnp.where(core == 1, 0, 2)

    def pick(at_left, at_right, at_last, at_first, usual):
        return jnp.where(left, at_left, jnp.where(right, at_right, jnp.where(last, at_last, jnp.where(first, at_first, usual))))

    own_dev, own_slot = pick(0, 15, 7, 8, near), pick(0, 2, 2, 0, near_slot)
    off_from = pick(1, 1, 2, 0, 1)

    neighbours = [(dt, dh) for dt in (-1, 0, 1) for dh in (-1, 0, 1) if dt or dh]

    def exists(dt, dh):
        return (t + dt >= 0) & (t + dt <= 15) & (h + dh >= 0) & (h + dh <= 7)

    barrier = pltpu.get_barrier_semaphore()

    def greet(frame, row):
        pl.semaphore_signal(barrier, inc=1, device_id=(frame, row), device_id_type=MESH)

    targets = (relay | bound).astype(jnp.int32) + z_to.astype(jnp.int32)
    for dt, dh in neighbours:
        targets = targets + exists(dt, dh).astype(jnp.int32)

        @pl.when(exists(dt, dh))
        def _():
            greet(t + dt, h + dh)

    @pl.when(relay | bound)
    def _():
        greet(pick(15, 0, 8, 7, 0), h)

    @pl.when(z_from)
    def _():
        greet(*z_src)

    pl.semaphore_wait(barrier, targets)

    def part(a, s, k):
        u, piece = k // PIECES, k % PIECES
        size = tiles.shape[3] // PIECES
        return tiles.at[a, s, u, pl.ds(piece * size, size)]

    def remote(src, dst, send, recv, device):
        return pltpu.make_async_remote_copy(
            src_ref=src, dst_ref=dst, send_sem=send, recv_sem=recv, device_id=device, device_id_type=MESH
        )

    def swap(k):
        return remote(part(1, 0, k), part(1, 1, k), sent.at[0], swap_recv.at[k], (t, other))

    def along_z(k):
        return remote(part(1, 1, k), part(1, 2, k), sent.at[1], z_recv.at[k], z_dst)

    def side_z(k):
        return remote(part(off_here, 1, k), part(off_here, 2, k), sent.at[2], off_recv.at[2, k], z_dst)

    def to_chip(s, k):
        return remote(part(1, s, k), part(chip_there, s, k), sent.at[3 + s], chip_recv.at[s, k // EARLY], chip_dev)

    def off_chip(s, k):
        frame, slot = (near, near_slot) if s else (own_dev, own_slot)
        return remote(part(off_from, s, k), part(slot, s, k), sent.at[6 + s], off_recv.at[s, k], (frame, h))

    def arrive(s, k):
        remote(part(1, s, k), part(off_here, s, k), sent.at[6], off_recv.at[s, k], chip_dev).wait_recv()

    def arrive_chip(s, late):
        both = tiles.at[chip_here, s, pl.ds(2 * late, 2)]
        remote(both, both, sent.at[3], chip_recv.at[s, late], chip_dev).wait_recv()

    def row_stats(dt, dh):
        a = 1 - dt
        s = jnp.where(odd == (dh + 1) // 2, 2, 1) * dh * dh
        return remote(stats.at[1, 0], stats.at[a, s], stats_send.at[a, dh + 1], stats_recv.at[a, s], (t + dt, h + dh))

    def spread(s, k):
        @pl.when(~(relay | bound) if s == 2 else ~relay)
        def _():
            off_chip(s, k).start()

        to_chip(s, k).start()

    def begin(k):
        swap(k).start()
        spread(0, k)

    def on_swap(k):
        swap(k).wait_recv()

        @pl.when(z_to)
        def _():
            along_z(k).start()

        spread(1, k)

    def on_z(k):
        @pl.when(z_from)
        def _():
            along_z(k).wait_recv()
            spread(2, k)

    def on_relay(k):
        arrive(0, k)
        off_chip(0, k).start()

    def on_side(k):
        arrive(1, k)

        @pl.when(z_to)
        def _():
            side_z(k).start()

    for copy in copies:
        copy.wait()
    for k in range(4):
        begin(k)

    clip = clip_ref[0]

    def columns(n):
        return slice(n * dim, (n + 1) * dim)

    row_max[...] = jnp.full(row_max.shape, NEGATIVE, jnp.float32)
    for ref in (acc, grad, row_sum, row_dot, key_acc, value_acc):
        ref[...] = jnp.zeros(ref.shape, ref.dtype)
    stats[1, 0] = jnp.zeros(stats.shape[2:], jnp.float32)
    for n in range(HEADS):
        out_grad_t[n] = tiles[1, 0, G, :, columns(n)].astype(jnp.float32).T

    EVENTS = (
        {
            2: [(on_swap, 0)],
            3: [(on_swap, 1), (on_z, 0), (on_swap, 2), (on_swap, 3)],
            4: [(on_z, 1), (begin, 4), (begin, 5)],
            5: [(on_z, 2)],
            6: [(on_z, 3)],
            7: [(begin, 6), (begin, 7), (on_swap, 4)],
            8: [(on_swap, 5)],
            9: [(on_z, 4), (on_swap, 6)],
            10: [(on_z, 5), (on_swap, 7)],
            13: [(on_z, 6)],
            14: [(on_z, 7)],
        },
        {
            2: [(on_swap, 0), (on_swap, 1), (on_z, 0), (on_swap, 2), (on_z, 1), (on_swap, 3)],
            3: [(on_z, 2), (begin, 4), (begin, 5), (on_side, 0)],
            4: [(on_side, 1), (on_z, 3), (on_side, 2)],
            5: [(on_side, 3)],
            6: [(begin, 6), (begin, 7)],
            7: [(on_swap, 4)],
            8: [(on_swap, 5)],
            10: [(on_swap, 6), (on_z, 4)],
            11: [(on_z, 5), (on_swap, 7)],
            12: [(on_side, 4), (on_side, 5)],
            14: [(on_side, 6), (on_z, 6)],
            15: [(on_z, 7), (on_side, 7)],
        },
        {
            2: [(on_relay, 0), (on_relay, 1), (on_swap, 0), (on_relay, 2), (on_relay, 3), (on_swap, 1), (on_z, 0), (on_swap, 2), (on_z, 1), (on_swap, 3), (begin, 4), (begin, 5)],
            4: [(on_z, 2), (on_relay, 4), (on_z, 3)],
            5: [(begin, 6), (begin, 7), (on_relay, 5)],
            6: [(on_swap, 4)],
            7: [(on_swap, 5)],
            8: [(on_relay, 6), (on_relay, 7), (on_z, 4), (on_z, 5), (on_swap, 6)],
            9: [(on_swap, 7)],
            10: [(on_z, 6)],
            11: [(on_z, 7)],
        },
    )
    WORDS = (
        (172066848, 379887846, 586692044, 658099826),
        (174197792, 379887842, 521679278, 658099826),
        (241306656, 551988553, 658099825, 658099827),
    )
    STEPS = 20

    kinds = (~(relay | bound), bound, relay)

    def events_at(step):
        for mine, events in zip(kinds, EVENTS):
            if step in events:
                @pl.when(mine)
                def _():
                    for entry in events[step]:
                        entry[0](*entry[1:])

    def dispatch(step, low, high):
        if high - low == 1:
            events_at(low)
        elif high > low:
            middle = (low + high) // 2

            @pl.when(step < middle)
            def _():
                dispatch(step, low, middle)

            @pl.when(step >= middle)
            def _():
                dispatch(step, middle, high)

    def word(i):
        return jnp.where(relay, WORDS[2][i], jnp.where(bound, WORDS[1][i], WORDS[0][i]))

    def queries_side(a, s, related):
        heads = range(HEADS)
        key = [tiles[a, s, K, :, columns(n)] for n in heads]
        value = [tiles[a, s, V, :, columns(n)] for n in heads]
        scores = [nt(key[n], tiles[1, 0, Q, :, columns(n)]) for n in heads]
        grad_weights = [nt(value[n], tiles[1, 0, G, :, columns(n)]) for n in heads]
        key_t = [key[n].T for n in heads]
        both_t = [jnp.concatenate([value[n].T, key_t[n]], axis=0) for n in heads]
        fades, raised, totals, dots = [], [], [], []
        for n in heads:
            top = jnp.where(related, jnp.max(scores[n], axis=0, keepdims=True) * to_log2, NEGATIVE)
            old_max = row_max[n]
            new_max = jnp.maximum(old_max, top)
            fades.append(jnp.exp2(old_max - new_max))
            raised.append(jnp.exp2(scores[n] * to_log2 - jnp.where(related, new_max, -NEGATIVE)))
            totals.append(row_sum[n] * fades[n] + jnp.sum(raised[n], axis=0, keepdims=True))
            row_max[n] = new_max
            row_sum[n] = totals[n]
        for n in heads:
            old = acc[n]
            new = old * fades[n] + nn(both_t[n], raised[n].astype(jnp.bfloat16))
            dots.append(jnp.sum(out_grad_t[n] * new[:dim], axis=0, keepdims=True) / totals[n])
            grad[n] = (grad[n] - (dots[n] - row_dot[n]) * old[dim:]) * fades[n]
            acc[n] = new
            row_dot[n] = dots[n]
        for n in heads:
            inner = (raised[n] * (grad_weights[n] - dots[n])).astype(jnp.bfloat16)
            grad[n] += nn(key_t[n], inner)

    def finish_queries():
        finish = []
        for n in range(HEADS):
            total = row_sum[n]
            sums = acc[n]
            attended = (sums[:dim] / total).astype(jnp.bfloat16).astype(jnp.float32)
            dot = jnp.sum(out_grad_t[n] * attended, axis=0, keepdims=True)
            stats[1, 0, n : n + 1] = row_max[n] + jnp.log2(total)
            stats[1, 0, HEADS + n : HEADS + n + 1] = dot
            finish.append((dot, total, sums, attended))
        for dt, dh in neighbours:
            @pl.when(exists(dt, dh))
            def _():
                row_stats(dt, dh).start()

        for n in range(HEADS):
            dot, total, sums, attended = finish[n]
            out_ref[0, :, columns(n)] = attended.T.astype(jnp.bfloat16)
            own_grad = (grad[n] - (dot - row_dot[n]) * sums[dim:]) * (scale / total)
            out_ref[1, :, columns(n)] = own_grad.T.astype(jnp.bfloat16)

    def keys_side(a, s, related):
        for n in range(HEADS):
            own_k, own_v = tiles[1, 0, K, :, columns(n)], tiles[1, 0, V, :, columns(n)]
            query, out_grad = tiles[a, s, Q, :, columns(n)], tiles[a, s, G, :, columns(n)]
            log_total = jnp.where(related, stats[a, s, n : n + 1], -NEGATIVE)
            dot = stats[a, s, HEADS + n : HEADS + n + 1]
            weights = jnp.exp2(nt(own_k, query) * to_log2 - log_total)
            inner = (weights * (nt(own_v, out_grad) - dot)).astype(jnp.bfloat16)
            value_acc[n] += nn(weights.astype(jnp.bfloat16), out_grad)
            key_acc[n] += nn(inner, query)

    def do_step(step, left_words):
        dispatch(step, 0, STEPS)
        now, later = left_words[0], left_words[1:]
        digit = now % 32
        kind = (digit >= 9).astype(jnp.int32) + (digit >= 10).astype(jnp.int32) + (digit >= 19).astype(jnp.int32)
        tile = digit % 10
        s, o = tile // 3, tile % 3
        a = jnp.where(o == 0, 1, jnp.where(o == 1, chip_here, off_here))
        there = ((s < 2) | z_from) & ((o < 2) | ~relay)
        related = ((t + a - 1) >= clip) == (t >= clip)
        waits = (o == 2) & ~(bound & (s == 1))

        @pl.when(there & (kind == QUERIES))
        def _():
            @pl.when(o == 1)
            def _():
                arrive_chip(s, 0)

            @pl.when(waits)
            def _():
                for k in range(EARLY):
                    arrive(s, k)

            queries_side(a, s, related)

        @pl.when(kind == FINISH)
        def _():
            finish_queries()

        @pl.when(there & (kind == KEYS))
        def _():
            @pl.when(o == 1)
            def _():
                arrive_chip(s, 1)

            @pl.when(waits)
            def _():
                for k in range(EARLY, CHUNKS):
                    arrive(s, k)

            @pl.when((s > 0) | (o > 0))
            def _():
                remote(stats.at[1, 0], stats.at[a, s], stats_send.at[1, 1], stats_recv.at[a, s], chip_dev).wait_recv()

            keys_side(a, s, related)

        turn = step % 6 == 5
        return tuple(
            jnp.where(turn, after, before) for before, after in zip((now // 32,) + later, later + (jnp.int32(0),))
        )

    lax.fori_loop(0, STEPS, do_step, tuple(word(i) for i in range(len(WORDS[0]))))

    for n in range(HEADS):
        out_ref[2, :, columns(n)] = (key_acc[n] * scale).astype(jnp.bfloat16)
        out_ref[3, :, columns(n)] = value_acc[n].astype(jnp.bfloat16)

    def drain(place):
        whole = tiles.at[1, 0]
        remote(whole, whole, sent.at[place], sent.at[place], chip_dev).wait_send()

    for place in (0, 3, 4, 6):
        drain(place)
    for place, used in ((1, z_to), (2, z_to & bound), (5, z_from), (7, ~relay), (8, z_from & ~(relay | bound))):
        @pl.when(used)
        def _():
            drain(place)

    for dt, dh in neighbours:
        @pl.when(exists(dt, dh))
        def _():
            row_stats(dt, dh).wait_send()


def shards(queries, key_states, value_states, out_grad, clip_start):
    rows, channels = queries.shape[-2:]
    dim = channels // HEADS
    flat = [x.reshape(rows, channels) for x in (queries, key_states, value_states, out_grad)]
    vmem = pl.BlockSpec(memory_space=pltpu.VMEM)
    outs = pl.pallas_call(
        kernel,
        out_shape=jax.ShapeDtypeStruct((4, rows, channels), jnp.bfloat16),
        in_specs=[pl.BlockSpec(memory_space=pltpu.SMEM)] + [pl.BlockSpec(memory_space=pltpu.HBM)] * 4,
        out_specs=vmem,
        scratch_shapes=[
            pltpu.VMEM((3, 3, 4, rows, channels), jnp.bfloat16),
            pltpu.VMEM((3, 3, 8, rows), jnp.float32),
            pltpu.VMEM((HEADS, dim, rows), jnp.float32),
            pltpu.VMEM((HEADS, 2 * dim, rows), jnp.float32),
            pltpu.VMEM((HEADS, dim, rows), jnp.float32),
            pltpu.VMEM((HEADS, 1, rows), jnp.float32),
            pltpu.VMEM((HEADS, 1, rows), jnp.float32),
            pltpu.VMEM((HEADS, 1, rows), jnp.float32),
            pltpu.VMEM((HEADS, rows, dim), jnp.float32),
            pltpu.VMEM((HEADS, rows, dim), jnp.float32),
            pltpu.SemaphoreType.DMA((4,)),
            pltpu.SemaphoreType.DMA((9,)),
            pltpu.SemaphoreType.DMA((CHUNKS,)),
            pltpu.SemaphoreType.DMA((CHUNKS,)),
            pltpu.SemaphoreType.DMA((3, 2)),
            pltpu.SemaphoreType.DMA((3, CHUNKS)),
            pltpu.SemaphoreType.DMA((3, 3)),
            pltpu.SemaphoreType.DMA((3, 3)),
        ],
        compiler_params=pltpu.CompilerParams(
            collective_id=0, has_side_effects=True, vmem_limit_bytes=64 * 2**20
        ),
        name="tile_attention",
    )(clip_start, *flat)
    return tuple(outs[i].reshape(queries.shape) for i in range(4))


def solution(mesh):
    spec = P("tm", "height", None, None, None)
    return jax.shard_map(
        shards, mesh=mesh, in_specs=(spec,) * 4 + (P(),), out_specs=(spec,) * 4, check_vma=False
    )
```

```python
import jax
import jax.numpy as jnp
from jax import lax
from jax.experimental import pallas as pl
from jax.experimental.pallas import tpu as pltpu
from jax.sharding import PartitionSpec as P

HEADS = 2
LOG2E = 1.4426950408889634
NEGATIVE = -1e30
MESH = pl.DeviceIdType.MESH
QUERIES, FINISH, KEYS, NOTHING = range(4)
K, V, Q, G = range(4)
PIECES = 3
EARLY = 2 * PIECES
CHUNKS = 4 * PIECES


def nt(left, right):
    return lax.dot_general(left, right, (((1,), (1,)), ((), ())), preferred_element_type=jnp.float32)


def nn(left, right):
    return jnp.dot(left, right, preferred_element_type=jnp.float32)


def kernel(
    clip_ref, q_in, k_in, v_in, g_in, out_ref,
    tiles, stats, out_grad_t, acc, grad, row_max, row_sum, row_dot, key_acc, value_acc,
    local_sem, sent, swap_recv, z_recv, chip_recv, off_recv, stats_send, stats_recv,
):
    t = lax.axis_index("tm")
    h = lax.axis_index("height")
    core, odd, z = t % 2, h % 2, h // 2
    dim = q_in.shape[-1] // HEADS
    scale = dim ** (-0.5)
    to_log2 = scale * LOG2E

    copies = [pltpu.make_async_copy(ref, tiles.at[1, 0, u], local_sem.at[u]) for u, ref in enumerate((k_in, v_in, q_in, g_in))]
    for copy in copies:
        copy.start()

    first, last, left, right = t == 0, t == 15, t == 7, t == 8
    relay, bound = first | last, left | right
    other = h + 1 - 2 * odd
    chip_dev = (t + 1 - 2 * core, h)
    z_to = jnp.where(odd == 0, z < 3, z > 0)
    z_from = jnp.where(odd == 0, z > 0, z < 3)
    z_dst = (t, h + 2 - 4 * odd)
    z_src = (t, h - 2 + 4 * odd)
    chip_there = jnp.where(core == 0, 0, 2)
    chip_here = 2 - chip_there
    off_here = chip_there
    near = jnp.where(core == 1, t + 1, t - 1)
    near_slot = jnp.where(core == 1, 0, 2)

    def pick(at_left, at_right, at_last, at_first, usual):
        return jnp.where(left, at_left, jnp.where(right, at_right, jnp.where(last, at_last, jnp.where(first, at_first, usual))))

    own_dev, own_slot = pick(0, 15, 7, 8, near), pick(0, 2, 2, 0, near_slot)
    off_from = pick(1, 1, 2, 0, 1)

    neighbours = [(dt, dh) for dt in (-1, 0, 1) for dh in (-1, 0, 1) if dt or dh]

    def exists(dt, dh):
        return (t + dt >= 0) & (t + dt <= 15) & (h + dh >= 0) & (h + dh <= 7)

    barrier = pltpu.get_barrier_semaphore()

    def greet(frame, row):
        pl.semaphore_signal(barrier, inc=1, device_id=(frame, row), device_id_type=MESH)

    targets = (relay | bound).astype(jnp.int32) + z_to.astype(jnp.int32)
    for dt, dh in neighbours:
        targets = targets + exists(dt, dh).astype(jnp.int32)

        @pl.when(exists(dt, dh))
        def _():
            greet(t + dt, h + dh)

    @pl.when(relay | bound)
    def _():
        greet(pick(15, 0, 8, 7, 0), h)

    @pl.when(z_from)
    def _():
        greet(*z_src)

    pl.semaphore_wait(barrier, targets)

    def part(a, s, k):
        u, piece = k // PIECES, k % PIECES
        size = tiles.shape[3] // PIECES
        return tiles.at[a, s, u, pl.ds(piece * size, size)]

    def remote(src, dst, send, recv, device):
        return pltpu.make_async_remote_copy(
            src_ref=src, dst_ref=dst, send_sem=send, recv_sem=recv, device_id=device, device_id_type=MESH
        )

    def swap(k):
        return remote(part(1, 0, k), part(1, 1, k), sent.at[0], swap_recv.at[k], (t, other))

    def along_z(k):
        return remote(part(1, 1, k), part(1, 2, k), sent.at[1], z_recv.at[k], z_dst)

    def side_z(k):
        return remote(part(off_here, 1, k), part(off_here, 2, k), sent.at[2], off_recv.at[2, k], z_dst)

    def to_chip(s, k):
        return remote(part(1, s, k), part(chip_there, s, k), sent.at[3 + s], chip_recv.at[s, k // EARLY], chip_dev)

    def off_chip(s, k):
        frame, slot = (near, near_slot) if s else (own_dev, own_slot)
        return remote(part(off_from, s, k), part(slot, s, k), sent.at[6 + s], off_recv.at[s, k], (frame, h))

    def arrive(s, k):
        remote(part(1, s, k), part(off_here, s, k), sent.at[6], off_recv.at[s, k], chip_dev).wait_recv()

    def arrive_chip(s, late):
        both = tiles.at[chip_here, s, pl.ds(2 * late, 2)]
        remote(both, both, sent.at[3], chip_recv.at[s, late], chip_dev).wait_recv()

    def row_stats(dt, dh):
        a = 1 - dt
        s = jnp.where(odd == (dh + 1) // 2, 2, 1) * dh * dh
        return remote(stats.at[1, 0], stats.at[a, s], stats_send.at[a, dh + 1], stats_recv.at[a, s], (t + dt, h + dh))

    def spread(s, k):
        @pl.when(~(relay | bound) if s == 2 else ~relay)
        def _():
            off_chip(s, k).start()

        to_chip(s, k).start()

    def begin(k):
        swap(k).start()
        spread(0, k)

    def on_swap(k):
        swap(k).wait_recv()

        @pl.when(z_to)
        def _():
            along_z(k).start()

        spread(1, k)

    def on_z(k):
        @pl.when(z_from)
        def _():
            along_z(k).wait_recv()
            spread(2, k)

    def on_relay(k):
        arrive(0, k)
        off_chip(0, k).start()

    def on_side(k):
        arrive(1, k)

        @pl.when(z_to)
        def _():
            side_z(k).start()

    for copy in copies:
        copy.wait()
    for k in range(6):
        begin(k)

    clip = clip_ref[0]

    def columns(n):
        return slice(n * dim, (n + 1) * dim)

    row_max[...] = jnp.full(row_max.shape, NEGATIVE, jnp.float32)
    for ref in (acc, grad, row_sum, row_dot, key_acc, value_acc):
        ref[...] = jnp.zeros(ref.shape, ref.dtype)
    stats[1, 0] = jnp.zeros(stats.shape[2:], jnp.float32)
    for n in range(HEADS):
        out_grad_t[n] = tiles[1, 0, G, :, columns(n)].astype(jnp.float32).T

    EVENTS = (
        {
            2: [(on_swap, 0), (on_swap, 1)],
            3: [(on_swap, 2), (on_z, 0), (on_swap, 3), (on_z, 1), (on_swap, 4), (begin, 6), (begin, 7), (begin, 8), (on_z, 2), (on_swap, 5)],
            4: [(on_z, 3)],
            5: [(on_z, 4), (on_swap, 6), (on_z, 5)],
            6: [(begin, 9), (begin, 10), (begin, 11), (on_swap, 7), (on_swap, 8), (on_z, 6)],
            8: [(on_z, 7), (on_swap, 9), (on_z, 8), (on_swap, 10)],
            9: [(on_swap, 11)],
            10: [(on_z, 9)],
            11: [(on_z, 10), (on_z, 11)],
        },
        {
            2: [(on_swap, 0), (on_swap, 1), (on_swap, 2), (on_z, 0), (on_swap, 3), (on_z, 1), (on_swap, 4), (on_z, 2), (on_swap, 5)],
            3: [(on_z, 3), (on_side, 0), (on_side, 1)],
            4: [(on_z, 4), (begin, 6), (begin, 7), (begin, 8), (on_side, 2), (on_z, 5)],
            5: [(on_side, 3)],
            6: [(on_side, 4), (begin, 9), (begin, 10), (begin, 11), (on_side, 5), (on_swap, 6)],
            7: [(on_swap, 7)],
            8: [(on_swap, 8)],
            9: [(on_swap, 9), (on_z, 6)],
            10: [(on_swap, 10), (on_z, 7), (on_swap, 11), (on_side, 6)],
            11: [(on_z, 8), (on_side, 7), (on_side, 8)],
            12: [(on_z, 9), (on_side, 9)],
            13: [(on_z, 10)],
            14: [(on_z, 11), (on_side, 10)],
            15: [(on_side, 11)],
        },
        {
            2: [(on_relay, 0), (on_relay, 1), (on_swap, 0), (on_relay, 2), (on_relay, 3), (on_swap, 1), (on_relay, 4), (on_relay, 5), (on_swap, 2), (on_z, 0), (on_swap, 3), (on_z, 1), (on_z, 2), (on_swap, 4), (begin, 6), (begin, 7), (begin, 8), (on_swap, 5)],
            3: [(on_z, 3)],
            4: [(on_z, 4), (on_z, 5)],
            5: [(begin, 9), (begin, 10), (begin, 11)],
            6: [(on_relay, 6), (on_relay, 7)],
            7: [(on_swap, 6), (on_relay, 8), (on_swap, 7)],
            8: [(on_relay, 9), (on_swap, 8), (on_z, 6), (on_relay, 10), (on_relay, 11), (on_swap, 9), (on_z, 7), (on_swap, 10), (on_swap, 11), (on_z, 8)],
            9: [(on_z, 9)],
            10: [(on_z, 10), (on_z, 11)],
        },
    )
    WORDS = (
        (205621280, 379887783, 587611597, 658099826),
        (241306656, 379887778, 587706798, 658099826),
        (241306656, 486976841, 658099825, 658099827),
    )
    STEPS = 20

    kinds = (~(relay | bound), bound, relay)

    def events_at(step):
        for mine, events in zip(kinds, EVENTS):
            if step in events:
                @pl.when(mine)
                def _():
                    for entry in events[step]:
                        entry[0](*entry[1:])

    def dispatch(step, low, high):
        if high - low == 1:
            events_at(low)
        elif high > low:
            middle = (low + high) // 2

            @pl.when(step < middle)
            def _():
                dispatch(step, low, middle)

            @pl.when(step >= middle)
            def _():
                dispatch(step, middle, high)

    def word(i):
        return jnp.where(relay, WORDS[2][i], jnp.where(bound, WORDS[1][i], WORDS[0][i]))

    def queries_side(a, s, related):
        heads = range(HEADS)
        key = [tiles[a, s, K, :, columns(n)] for n in heads]
        value = [tiles[a, s, V, :, columns(n)] for n in heads]
        scores = [nt(key[n], tiles[1, 0, Q, :, columns(n)]) for n in heads]
        grad_weights = [nt(value[n], tiles[1, 0, G, :, columns(n)]) for n in heads]
        key_t = [key[n].T for n in heads]
        both_t = [jnp.concatenate([value[n].T, key_t[n]], axis=0) for n in heads]
        fades, raised, totals, dots = [], [], [], []
        for n in heads:
            top = jnp.where(related, jnp.max(scores[n], axis=0, keepdims=True) * to_log2, NEGATIVE)
            old_max = row_max[n]
            new_max = jnp.maximum(old_max, top)
            fades.append(jnp.exp2(old_max - new_max))
            raised.append(jnp.exp2(scores[n] * to_log2 - jnp.where(related, new_max, -NEGATIVE)))
            totals.append(row_sum[n] * fades[n] + jnp.sum(raised[n], axis=0, keepdims=True))
            row_max[n] = new_max
            row_sum[n] = totals[n]
        for n in heads:
            old = acc[n]
            new = old * fades[n] + nn(both_t[n], raised[n].astype(jnp.bfloat16))
            dots.append(jnp.sum(out_grad_t[n] * new[:dim], axis=0, keepdims=True) / totals[n])
            grad[n] = (grad[n] - (dots[n] - row_dot[n]) * old[dim:]) * fades[n]
            acc[n] = new
            row_dot[n] = dots[n]
        for n in heads:
            inner = (raised[n] * (grad_weights[n] - dots[n])).astype(jnp.bfloat16)
            grad[n] += nn(key_t[n], inner)

    def finish_queries():
        finish = []
        for n in range(HEADS):
            total = row_sum[n]
            sums = acc[n]
            attended = (sums[:dim] / total).astype(jnp.bfloat16).astype(jnp.float32)
            dot = jnp.sum(out_grad_t[n] * attended, axis=0, keepdims=True)
            stats[1, 0, n : n + 1] = row_max[n] + jnp.log2(total)
            stats[1, 0, HEADS + n : HEADS + n + 1] = dot
            finish.append((dot, total, sums, attended))
        for dt, dh in neighbours:
            @pl.when(exists(dt, dh))
            def _():
                row_stats(dt, dh).start()

        for n in range(HEADS):
            dot, total, sums, attended = finish[n]
            out_ref[0, :, columns(n)] = attended.T.astype(jnp.bfloat16)
            own_grad = (grad[n] - (dot - row_dot[n]) * sums[dim:]) * (scale / total)
            out_ref[1, :, columns(n)] = own_grad.T.astype(jnp.bfloat16)

    def keys_side(a, s, related):
        for n in range(HEADS):
            own_k, own_v = tiles[1, 0, K, :, columns(n)], tiles[1, 0, V, :, columns(n)]
            query, out_grad = tiles[a, s, Q, :, columns(n)], tiles[a, s, G, :, columns(n)]
            log_total = jnp.where(related, stats[a, s, n : n + 1], -NEGATIVE)
            dot = stats[a, s, HEADS + n : HEADS + n + 1]
            weights = jnp.exp2(nt(own_k, query) * to_log2 - log_total)
            inner = (weights * (nt(own_v, out_grad) - dot)).astype(jnp.bfloat16)
            value_acc[n] += nn(weights.astype(jnp.bfloat16), out_grad)
            key_acc[n] += nn(inner, query)

    def do_step(step, left_words):
        dispatch(step, 0, STEPS)
        now, later = left_words[0], left_words[1:]
        digit = now % 32
        kind = (digit >= 9).astype(jnp.int32) + (digit >= 10).astype(jnp.int32) + (digit >= 19).astype(jnp.int32)
        tile = digit % 10
        s, o = tile // 3, tile % 3
        a = jnp.where(o == 0, 1, jnp.where(o == 1, chip_here, off_here))
        there = ((s < 2) | z_from) & ((o < 2) | ~relay)
        related = ((t + a - 1) >= clip) == (t >= clip)
        waits = (o == 2) & ~(bound & (s == 1))

        @pl.when(there & (kind == QUERIES))
        def _():
            @pl.when(o == 1)
            def _():
                arrive_chip(s, 0)

            @pl.when(waits)
            def _():
                for k in range(EARLY):
                    arrive(s, k)

            queries_side(a, s, related)

        @pl.when(kind == FINISH)
        def _():
            finish_queries()

        @pl.when(there & (kind == KEYS))
        def _():
            @pl.when(o == 1)
            def _():
                arrive_chip(s, 1)

            @pl.when(waits)
            def _():
                for k in range(EARLY, CHUNKS):
                    arrive(s, k)

            @pl.when((s > 0) | (o > 0))
            def _():
                remote(stats.at[1, 0], stats.at[a, s], stats_send.at[1, 1], stats_recv.at[a, s], chip_dev).wait_recv()

            keys_side(a, s, related)

        turn = step % 6 == 5
        return tuple(
            jnp.where(turn, after, before) for before, after in zip((now // 32,) + later, later + (jnp.int32(0),))
        )

    lax.fori_loop(0, STEPS, do_step, tuple(word(i) for i in range(len(WORDS[0]))))

    for n in range(HEADS):
        out_ref[2, :, columns(n)] = (key_acc[n] * scale).astype(jnp.bfloat16)
        out_ref[3, :, columns(n)] = value_acc[n].astype(jnp.bfloat16)

    def drain(place):
        whole = tiles.at[1, 0]
        remote(whole, whole, sent.at[place], sent.at[place], chip_dev).wait_send()

    for place in (0, 3, 4, 6):
        drain(place)
    for place, used in ((1, z_to), (2, z_to & bound), (5, z_from), (7, ~relay), (8, z_from & ~(relay | bound))):
        @pl.when(used)
        def _():
            drain(place)

    for dt, dh in neighbours:
        @pl.when(exists(dt, dh))
        def _():
            row_stats(dt, dh).wait_send()


def shards(queries, key_states, value_states, out_grad, clip_start):
    rows, channels = queries.shape[-2:]
    dim = channels // HEADS
    flat = [
        pltpu.with_memory_space_constraint(x.reshape(rows, channels), pltpu.HBM)
        for x in (queries, key_states, value_states, out_grad)
    ]
    vmem = pl.BlockSpec(memory_space=pltpu.VMEM)
    outs = pl.pallas_call(
        kernel,
        out_shape=pltpu.VMEM((4, rows, channels), jnp.bfloat16),
        in_specs=[pl.BlockSpec(memory_space=pltpu.SMEM)] + [pl.BlockSpec(memory_space=pltpu.HBM)] * 4,
        out_specs=vmem,
        scratch_shapes=[
            pltpu.VMEM((3, 3, 4, rows, channels), jnp.bfloat16),
            pltpu.VMEM((3, 3, 8, rows), jnp.float32),
            pltpu.VMEM((HEADS, dim, rows), jnp.float32),
            pltpu.VMEM((HEADS, 2 * dim, rows), jnp.float32),
            pltpu.VMEM((HEADS, dim, rows), jnp.float32),
            pltpu.VMEM((HEADS, 1, rows), jnp.float32),
            pltpu.VMEM((HEADS, 1, rows), jnp.float32),
            pltpu.VMEM((HEADS, 1, rows), jnp.float32),
            pltpu.VMEM((HEADS, rows, dim), jnp.float32),
            pltpu.VMEM((HEADS, rows, dim), jnp.float32),
            pltpu.SemaphoreType.DMA((4,)),
            pltpu.SemaphoreType.DMA((9,)),
            pltpu.SemaphoreType.DMA((CHUNKS,)),
            pltpu.SemaphoreType.DMA((CHUNKS,)),
            pltpu.SemaphoreType.DMA((3, 2)),
            pltpu.SemaphoreType.DMA((3, CHUNKS)),
            pltpu.SemaphoreType.DMA((3, 3)),
            pltpu.SemaphoreType.DMA((3, 3)),
        ],
        compiler_params=pltpu.CompilerParams(
            collective_id=0, has_side_effects=True, vmem_limit_bytes=48 * 2**20
        ),
        name="tile_attention",
    )(clip_start, *flat)
    return tuple(outs[i].reshape(queries.shape) for i in range(4))


def solution(mesh):
    spec = P("tm", "height", None, None, None)
    return jax.shard_map(
        shards, mesh=mesh, in_specs=(spec,) * 4 + (P(),), out_specs=(spec,) * 4, check_vma=False
    )
```

```python
import jax
import jax.numpy as jnp
from jax import lax
from jax.experimental import pallas as pl
from jax.experimental.pallas import tpu as pltpu
from jax.sharding import PartitionSpec as P

HEADS = 2
LOG2E = 1.4426950408889634
NEGATIVE = -1e30
MESH = pl.DeviceIdType.MESH
FINISH, KEYS, PAIRS, NOTHING = 9, 10, 19, 22
K, V, Q, G = range(4)
PIECES = 3
EARLY = 2 * PIECES
CHUNKS = 4 * PIECES
DIRECT = (9, 10, 11,)


def nt(left, right):
    return lax.dot_general(left, right, (((1,), (1,)), ((), ())), preferred_element_type=jnp.float32)


def nn(left, right):
    return jnp.dot(left, right, preferred_element_type=jnp.float32)


def kernel(
    clip_ref, q_in, k_in, v_in, g_in, out_ref,
    tiles, stats, out_grad_t, acc, grad, row_max, row_sum, row_dot, key_acc, value_acc,
    local_sem, sent, swap_recv, z_recv, chip_recv, off_recv, stats_send, stats_recv,
):
    t = lax.axis_index("tm")
    h = lax.axis_index("height")
    core, odd, z = t % 2, h % 2, h // 2
    dim = q_in.shape[-1] // HEADS
    scale = dim ** (-0.5)
    to_log2 = scale * LOG2E

    copies = [pltpu.make_async_copy(ref, tiles.at[1, 0, u], local_sem.at[u]) for u, ref in enumerate((k_in, v_in, q_in, g_in))]
    for copy in copies:
        copy.start()

    first, last, left, right = t == 0, t == 15, t == 7, t == 8
    relay, bound = first | last, left | right
    other = h + 1 - 2 * odd
    chip_dev = (t + 1 - 2 * core, h)
    z_to = jnp.where(odd == 0, z < 3, z > 0)
    z_from = jnp.where(odd == 0, z > 0, z < 3)
    z_dst = (t, h + 2 - 4 * odd)
    z_src = (t, h - 2 + 4 * odd)
    chip_there = jnp.where(core == 0, 0, 2)
    chip_here = 2 - chip_there
    off_here = chip_there
    near = jnp.where(core == 1, t + 1, t - 1)
    near_slot = jnp.where(core == 1, 0, 2)

    def pick(at_left, at_right, at_last, at_first, usual):
        return jnp.where(left, at_left, jnp.where(right, at_right, jnp.where(last, at_last, jnp.where(first, at_first, usual))))

    own_dev, own_slot = pick(0, 15, 7, 8, near), pick(0, 2, 2, 0, near_slot)
    off_from = pick(1, 1, 2, 0, 1)

    neighbours = [(dt, dh) for dt in (-1, 0, 1) for dh in (-1, 0, 1) if dt or dh]

    def exists(dt, dh):
        return (t + dt >= 0) & (t + dt <= 15) & (h + dh >= 0) & (h + dh <= 7)

    barrier = pltpu.get_barrier_semaphore()

    def greet(frame, row):
        pl.semaphore_signal(barrier, inc=1, device_id=(frame, row), device_id_type=MESH)

    targets = (relay | bound).astype(jnp.int32) + z_to.astype(jnp.int32)
    for dt, dh in neighbours:
        targets = targets + exists(dt, dh).astype(jnp.int32)

        @pl.when(exists(dt, dh))
        def _():
            greet(t + dt, h + dh)

    @pl.when(relay | bound)
    def _():
        greet(pick(15, 0, 8, 7, 0), h)

    @pl.when(z_from)
    def _():
        greet(*z_src)

    pl.semaphore_wait(barrier, targets)

    def part(a, s, k):
        u, piece = k // PIECES, k % PIECES
        size = tiles.shape[3] // PIECES
        return tiles.at[a, s, u, pl.ds(piece * size, size)]

    def remote(src, dst, send, recv, device):
        return pltpu.make_async_remote_copy(
            src_ref=src, dst_ref=dst, send_sem=send, recv_sem=recv, device_id=device, device_id_type=MESH
        )

    def swap(k):
        return remote(part(1, 0, k), part(1, 1, k), sent.at[0], swap_recv.at[k], (t, other))

    def along_z(k):
        return remote(part(1, 1, k), part(1, 2, k), sent.at[1], z_recv.at[k], z_dst)

    def side_z(k):
        return remote(part(off_here, 1, k), part(off_here, 2, k), sent.at[2], off_recv.at[2, k], z_dst)

    def to_chip(s, k):
        return remote(part(1, s, k), part(chip_there, s, k), sent.at[3 + s], chip_recv.at[s, k // EARLY], chip_dev)

    def off_chip(s, k):
        frame, slot = (near, near_slot) if s else (own_dev, own_slot)
        return remote(part(off_from, s, k), part(slot, s, k), sent.at[6 + s], off_recv.at[s, k], (frame, h))

    def arrive(s, k):
        remote(part(1, s, k), part(off_here, s, k), sent.at[6], off_recv.at[s, k], chip_dev).wait_recv()

    def arrive_chip(s, late):
        both = tiles.at[chip_here, s, pl.ds(2 * late, 2)]
        remote(both, both, sent.at[3], chip_recv.at[s, late], chip_dev).wait_recv()

    def row_stats(dt, dh):
        a = 1 - dt
        s = jnp.where(odd == (dh + 1) // 2, 2, 1) * dh * dh
        return remote(stats.at[1, 0], stats.at[a, s], stats_send.at[a, dh + 1], stats_recv.at[a, s], (t + dt, h + dh))

    def spread(s, k):
        @pl.when(~(relay | bound) if s == 2 and k not in DIRECT else ~relay)
        def _():
            off_chip(s, k).start()

        to_chip(s, k).start()

    def begin(k):
        swap(k).start()

        @pl.when(~relay)
        def _():
            off_chip(0, k).start()

    def on_swap(k):
        swap(k).wait_recv()

        @pl.when(z_to)
        def _():
            along_z(k).start()

        spread(1, k)

    def on_z(k):
        @pl.when(z_from)
        def _():
            along_z(k).wait_recv()
            spread(2, k)

    def on_relay(k):
        arrive(0, k)
        off_chip(0, k).start()

    def on_side(k):
        arrive(1, k)

        @pl.when(z_to)
        def _():
            side_z(k).start()

    for copy in copies:
        copy.wait()
    for k in range(CHUNKS):
        if k in range(6):
            begin(k)
        to_chip(0, k).start()

    clip = clip_ref[0]

    def columns(n):
        return slice(n * dim, (n + 1) * dim)

    row_max[...] = jnp.full(row_max.shape, NEGATIVE, jnp.float32)
    for ref in (acc, grad, row_sum, row_dot, key_acc, value_acc):
        ref[...] = jnp.zeros(ref.shape, ref.dtype)
    stats[1, 0] = jnp.zeros(stats.shape[2:], jnp.float32)
    for n in range(HEADS):
        out_grad_t[n] = tiles[1, 0, G, :, columns(n)].astype(jnp.float32).T

    EVENTS = (
        {
            2: [(on_swap, 0), (on_swap, 1)],
            3: [(on_swap, 2), (on_z, 0), (on_swap, 3), (on_z, 1), (on_swap, 4), (on_swap, 5), (on_z, 2), (begin, 6), (begin, 7), (begin, 8)],
            4: [(on_z, 3)],
            5: [(on_z, 4), (on_swap, 6)],
            6: [(on_z, 5), (on_swap, 7), (begin, 9), (begin, 10), (begin, 11)],
            7: [(on_swap, 8), (on_z, 6)],
            8: [(on_z, 7), (on_swap, 9)],
            9: [(on_swap, 10)],
            10: [(on_z, 8), (on_swap, 11), (on_z, 9)],
            11: [(on_z, 10)],
            13: [(on_z, 11)],
        },
        {
            2: [(on_swap, 0), (on_swap, 1), (on_swap, 2), (on_z, 0), (on_swap, 3), (on_z, 1), (on_swap, 4), (on_z, 2), (on_swap, 5)],
            3: [(on_side, 0), (on_z, 3), (on_side, 1)],
            4: [(begin, 6), (begin, 7), (begin, 8), (on_side, 2), (on_z, 4), (on_side, 3), (on_z, 5)],
            5: [(on_side, 4)],
            6: [(on_side, 5), (begin, 9), (begin, 10), (begin, 11)],
            7: [(on_swap, 6), (on_swap, 7)],
            8: [(on_swap, 8)],
            9: [(on_swap, 9)],
            10: [(on_z, 6), (on_swap, 10), (on_z, 7), (on_swap, 11), (on_z, 8)],
            11: [(on_side, 6), (on_z, 9), (on_side, 7), (on_side, 8), (on_z, 10)],
            12: [(on_z, 11)],
        },
        {
            2: [(on_relay, 0), (on_relay, 1), (on_swap, 0), (on_relay, 2), (on_relay, 3), (on_swap, 1), (on_relay, 4), (on_relay, 5), (on_swap, 2), (on_z, 0), (on_swap, 3), (on_z, 1), (on_swap, 4), (on_z, 2), (on_swap, 5)],
            3: [(begin, 6), (begin, 7), (begin, 8), (on_z, 3)],
            4: [(on_z, 4), (on_z, 5)],
            5: [(begin, 9), (begin, 10), (begin, 11), (on_relay, 6)],
            6: [(on_relay, 7), (on_relay, 8), (on_swap, 6), (on_swap, 7)],
            7: [(on_swap, 8), (on_relay, 9), (on_swap, 9), (on_relay, 10), (on_relay, 11), (on_z, 6), (on_swap, 10)],
            8: [(on_z, 7), (on_swap, 11), (on_z, 8), (on_z, 9), (on_z, 10)],
            9: [(on_z, 11)],
        },
    )
    WORDS = (
        (172066848, 422879462, 761878004),
        (73534496, 691314855, 761877996),
        (241306656, 761975401, 762010326),
    )
    STEPS = 17

    kinds = (~(relay | bound), bound, relay)

    def events_at(step):
        for mine, events in zip(kinds, EVENTS):
            if step in events:
                @pl.when(mine)
                def _():
                    for entry in events[step]:
                        entry[0](*entry[1:])

    def dispatch(step, low, high):
        if high - low == 1:
            events_at(low)
        elif high > low:
            middle = (low + high) // 2

            @pl.when(step < middle)
            def _():
                dispatch(step, low, middle)

            @pl.when(step >= middle)
            def _():
                dispatch(step, middle, high)

    def word(i):
        return jnp.where(relay, WORDS[2][i], jnp.where(bound, WORDS[1][i], WORDS[0][i]))

    def queries_side(a, s, related):
        heads = range(HEADS)
        key = [tiles[a, s, K, :, columns(n)] for n in heads]
        value = [tiles[a, s, V, :, columns(n)] for n in heads]
        scores = [nt(key[n], tiles[1, 0, Q, :, columns(n)]) for n in heads]
        grad_weights = [nt(value[n], tiles[1, 0, G, :, columns(n)]) for n in heads]
        key_t = [key[n].T for n in heads]
        both_t = [jnp.concatenate([value[n].T, key_t[n]], axis=0) for n in heads]
        fades, raised, totals, dots = [], [], [], []
        for n in heads:
            top = jnp.where(related, jnp.max(scores[n], axis=0, keepdims=True) * to_log2, NEGATIVE)
            old_max = row_max[n]
            new_max = jnp.maximum(old_max, top)
            fades.append(jnp.exp2(old_max - new_max))
            raised.append(jnp.exp2(scores[n] * to_log2 - jnp.where(related, new_max, -NEGATIVE)))
            totals.append(row_sum[n] * fades[n] + jnp.sum(raised[n], axis=0, keepdims=True))
            row_max[n] = new_max
            row_sum[n] = totals[n]
        for n in heads:
            old = acc[n]
            new = old * fades[n] + nn(both_t[n], raised[n].astype(jnp.bfloat16))
            dots.append(jnp.sum(out_grad_t[n] * new[:dim], axis=0, keepdims=True) / totals[n])
            grad[n] = (grad[n] - (dots[n] - row_dot[n]) * old[dim:]) * fades[n]
            acc[n] = new
            row_dot[n] = dots[n]
        for n in heads:
            inner = (raised[n] * (grad_weights[n] - dots[n])).astype(jnp.bfloat16)
            grad[n] += nn(key_t[n], inner)

    def finish_queries():
        finish = []
        for n in range(HEADS):
            total = row_sum[n]
            sums = acc[n]
            attended = (sums[:dim] / total).astype(jnp.bfloat16).astype(jnp.float32)
            dot = jnp.sum(out_grad_t[n] * attended, axis=0, keepdims=True)
            stats[1, 0, n : n + 1] = row_max[n] + jnp.log2(total)
            stats[1, 0, HEADS + n : HEADS + n + 1] = dot
            finish.append((dot, total, sums, attended))
        for dt, dh in neighbours:
            @pl.when(exists(dt, dh))
            def _():
                row_stats(dt, dh).start()

        for n in range(HEADS):
            dot, total, sums, attended = finish[n]
            out_ref[0, :, columns(n)] = attended.T.astype(jnp.bfloat16)
            own_grad = (grad[n] - (dot - row_dot[n]) * sums[dim:]) * (scale / total)
            out_ref[1, :, columns(n)] = own_grad.T.astype(jnp.bfloat16)

    def keys_side(s, frames):
        for n in range(HEADS):
            own_k, own_v = tiles[1, 0, K, :, columns(n)], tiles[1, 0, V, :, columns(n)]
            to_value, to_key = [], []
            for a, counts in frames:
                query, out_grad = tiles[a, s, Q, :, columns(n)], tiles[a, s, G, :, columns(n)]
                log_total = jnp.where(counts, stats[a, s, n : n + 1], -NEGATIVE)
                dot = stats[a, s, HEADS + n : HEADS + n + 1]
                weights = jnp.exp2(nt(own_k, query) * to_log2 - log_total)
                inner = (weights * (nt(own_v, out_grad) - dot)).astype(jnp.bfloat16)
                to_value.append(nn(weights.astype(jnp.bfloat16), out_grad))
                to_key.append(nn(inner, query))
            value_acc[n] += sum(to_value[1:], to_value[0])
            key_acc[n] += sum(to_key[1:], to_key[0])

    def frame(o):
        a = jnp.where(o == 0, 1, jnp.where(o == 1, chip_here, off_here))
        return a, ((t + a - 1) >= clip) == (t >= clip)

    def arrive_stats(a, s):
        remote(stats.at[1, 0], stats.at[a, s], stats_send.at[1, 1], stats_recv.at[a, s], chip_dev).wait_recv()

    def do_step(step, left_words):
        dispatch(step, 0, STEPS)
        now, later = left_words[0], left_words[1:]
        digit = now % 32
        s, o = digit // 3, digit % 3

        @pl.when((digit < 9) & ((s < 2) | z_from) & ((o < 2) | ~relay))
        def _():
            @pl.when(o == 1)
            def _():
                arrive_chip(s, 0)

            @pl.when((o == 2) & ~(bound & (s == 1)))
            def _():
                for k in range(EARLY):
                    arrive(s, k)

            queries_side(frame(o)[0], s, frame(o)[1])

        @pl.when(digit == FINISH)
        def _():
            finish_queries()

        single = digit - KEYS
        row, o = single // 3, single % 3

        @pl.when((digit >= KEYS) & (digit < PAIRS) & ((row < 2) | z_from) & ((o < 2) | ~relay))
        def _():
            @pl.when(o == 1)
            def _():
                arrive_chip(row, 1)

            @pl.when(o == 2)
            def _():
                for k in range(EARLY, CHUNKS):
                    if k in DIRECT:
                        arrive(row, k)
                    else:
                        @pl.when(~(bound & (row == 1)))
                        def _():
                            arrive(row, k)

            @pl.when(single > 0)
            def _():
                arrive_stats(frame(o)[0], row)

            keys_side(row, (frame(o),))

        pair = digit - PAIRS

        @pl.when((digit >= PAIRS) & (digit < NOTHING) & ((pair < 2) | z_from))
        def _():
            arrive_chip(pair, 1)
            arrive_stats(chip_here, pair)

            @pl.when(pair > 0)
            def _():
                arrive_stats(1, pair)

            keys_side(pair, (frame(0), frame(1)))

        turn = step % 6 == 5
        return tuple(
            jnp.where(turn, after, before) for before, after in zip((now // 32,) + later, later + (jnp.int32(0),))
        )

    lax.fori_loop(0, STEPS, do_step, tuple(word(i) for i in range(len(WORDS[0]))))

    for n in range(HEADS):
        out_ref[2, :, columns(n)] = (key_acc[n] * scale).astype(jnp.bfloat16)
        out_ref[3, :, columns(n)] = value_acc[n].astype(jnp.bfloat16)

    def drain(place, arrays=4):
        whole = tiles.at[1, 0, pl.ds(0, arrays)]
        remote(whole, whole, sent.at[place], sent.at[place], chip_dev).wait_send()

    direct = len(DIRECT) // PIECES
    usual = ~(relay | bound)
    for place in (0, 3, 4, 6):
        drain(place)
    for place, used, arrays in (
        (1, z_to, 4), (2, z_to & bound, 4 - direct), (5, z_from, 4), (7, ~relay, 4), (8, z_from & usual, 4), (8, z_from & bound, direct)
    ):
        if arrays:
            @pl.when(used)
            def _():
                drain(place, arrays)

    for dt, dh in neighbours:
        @pl.when(exists(dt, dh))
        def _():
            row_stats(dt, dh).wait_send()


def shards(queries, key_states, value_states, out_grad, clip_start):
    rows, channels = queries.shape[-2:]
    dim = channels // HEADS
    flat = [
        pltpu.with_memory_space_constraint(x.reshape(rows, channels), pltpu.HBM)
        for x in (queries, key_states, value_states, out_grad)
    ]
    vmem = pl.BlockSpec(memory_space=pltpu.VMEM)
    outs = pl.pallas_call(
        kernel,
        out_shape=pltpu.VMEM((4, rows, channels), jnp.bfloat16),
        in_specs=[pl.BlockSpec(memory_space=pltpu.SMEM)] + [pl.BlockSpec(memory_space=pltpu.HBM)] * 4,
        out_specs=vmem,
        scratch_shapes=[
            pltpu.VMEM((3, 3, 4, rows, channels), jnp.bfloat16),
            pltpu.VMEM((3, 3, 8, rows), jnp.float32),
            pltpu.VMEM((HEADS, dim, rows), jnp.float32),
            pltpu.VMEM((HEADS, 2 * dim, rows), jnp.float32),
            pltpu.VMEM((HEADS, dim, rows), jnp.float32),
            pltpu.VMEM((HEADS, 1, rows), jnp.float32),
            pltpu.VMEM((HEADS, 1, rows), jnp.float32),
            pltpu.VMEM((HEADS, 1, rows), jnp.float32),
            pltpu.VMEM((HEADS, rows, dim), jnp.float32),
            pltpu.VMEM((HEADS, rows, dim), jnp.float32),
            pltpu.SemaphoreType.DMA((4,)),
            pltpu.SemaphoreType.DMA((9,)),
            pltpu.SemaphoreType.DMA((CHUNKS,)),
            pltpu.SemaphoreType.DMA((CHUNKS,)),
            pltpu.SemaphoreType.DMA((3, 2)),
            pltpu.SemaphoreType.DMA((3, CHUNKS)),
            pltpu.SemaphoreType.DMA((3, 3)),
            pltpu.SemaphoreType.DMA((3, 3)),
        ],
        compiler_params=pltpu.CompilerParams(
            collective_id=0, has_side_effects=True, vmem_limit_bytes=48 * 2**20
        ),
        name="tile_attention",
    )(clip_start, *flat)
    return tuple(outs[i].reshape(queries.shape) for i in range(4))


def solution(mesh):
    spec = P("tm", "height", None, None, None)
    return jax.shard_map(
        shards, mesh=mesh, in_specs=(spec,) * 4 + (P(),), out_specs=(spec,) * 4, check_vma=False
    )
```

```python
import jax
import jax.numpy as jnp
from jax import lax
from jax.experimental import pallas as pl
from jax.experimental.pallas import tpu as pltpu
from jax.sharding import PartitionSpec as P

HEADS = 2
LOG2E = 1.4426950408889634
NEGATIVE = -1e30
MESH = pl.DeviceIdType.MESH
FINISH, KEYS, PAIRS, NOTHING = 9, 10, 19, 22
K, V, Q, G = range(4)
PIECES = 3
EARLY = 2 * PIECES
CHUNKS = 4 * PIECES
DIRECT = (9, 10, 11,)


def nt(left, right):
    return lax.dot_general(left, right, (((1,), (1,)), ((), ())), preferred_element_type=jnp.float32)


def nn(left, right):
    return jnp.dot(left, right, preferred_element_type=jnp.float32)


def kernel(
    clip_ref, q_in, k_in, v_in, g_in, out_ref,
    tiles, stats, out_grad_t, acc, grad, row_max, row_sum, row_dot, key_acc, value_acc,
    local_sem, sent, swap_recv, z_recv, chip_recv, off_recv, stats_send, stats_recv,
):
    t = lax.axis_index("tm")
    h = lax.axis_index("height")
    core, odd, z = t % 2, h % 2, h // 2
    dim = q_in.shape[-1] // HEADS
    scale = dim ** (-0.5)
    to_log2 = scale * LOG2E

    copies = [pltpu.make_async_copy(ref, tiles.at[1, 0, u], local_sem.at[u]) for u, ref in enumerate((k_in, v_in, q_in, g_in))]
    for copy in copies:
        copy.start()

    first, last, left, right = t == 0, t == 15, t == 7, t == 8
    relay, bound = first | last, left | right
    other = h + 1 - 2 * odd
    chip_dev = (t + 1 - 2 * core, h)
    z_to = jnp.where(odd == 0, z < 3, z > 0)
    z_from = jnp.where(odd == 0, z > 0, z < 3)
    z_dst = (t, h + 2 - 4 * odd)
    z_src = (t, h - 2 + 4 * odd)
    chip_there = jnp.where(core == 0, 0, 2)
    chip_here = 2 - chip_there
    off_here = chip_there
    near = jnp.where(core == 1, t + 1, t - 1)
    near_slot = jnp.where(core == 1, 0, 2)

    def pick(at_left, at_right, at_last, at_first, usual):
        return jnp.where(left, at_left, jnp.where(right, at_right, jnp.where(last, at_last, jnp.where(first, at_first, usual))))

    own_dev, own_slot = pick(0, 15, 7, 8, near), pick(0, 2, 2, 0, near_slot)
    off_from = pick(1, 1, 2, 0, 1)

    neighbours = [(dt, dh) for dt in (-1, 0, 1) for dh in (-1, 0, 1) if dt or dh]

    def exists(dt, dh):
        return (t + dt >= 0) & (t + dt <= 15) & (h + dh >= 0) & (h + dh <= 7)

    barrier = pltpu.get_barrier_semaphore()

    def greet(frame, row):
        pl.semaphore_signal(barrier, inc=1, device_id=(frame, row), device_id_type=MESH)

    targets = (relay | bound).astype(jnp.int32) + z_to.astype(jnp.int32)
    for dt, dh in neighbours:
        targets = targets + exists(dt, dh).astype(jnp.int32)

        @pl.when(exists(dt, dh))
        def _():
            greet(t + dt, h + dh)

    @pl.when(relay | bound)
    def _():
        greet(pick(15, 0, 8, 7, 0), h)

    @pl.when(z_from)
    def _():
        greet(*z_src)

    pl.semaphore_wait(barrier, targets)

    def part(a, s, k):
        u, piece = k // PIECES, k % PIECES
        size = tiles.shape[3] // PIECES
        return tiles.at[a, s, u, pl.ds(piece * size, size)]

    def remote(src, dst, send, recv, device):
        return pltpu.make_async_remote_copy(
            src_ref=src, dst_ref=dst, send_sem=send, recv_sem=recv, device_id=device, device_id_type=MESH
        )

    def swap(k):
        return remote(part(1, 0, k), part(1, 1, k), sent.at[0], swap_recv.at[k], (t, other))

    def along_z(k):
        return remote(part(1, 1, k), part(1, 2, k), sent.at[1], z_recv.at[k], z_dst)

    def side_z(k):
        return remote(part(off_here, 1, k), part(off_here, 2, k), sent.at[2], off_recv.at[2, k], z_dst)

    def to_chip(s, k):
        return remote(part(1, s, k), part(chip_there, s, k), sent.at[3 + s], chip_recv.at[s, k // EARLY], chip_dev)

    def off_chip(s, k):
        frame, slot = (near, near_slot) if s else (own_dev, own_slot)
        return remote(part(off_from, s, k), part(slot, s, k), sent.at[6 + s], off_recv.at[s, k], (frame, h))

    def arrive(s, k):
        remote(part(1, s, k), part(off_here, s, k), sent.at[6], off_recv.at[s, k], chip_dev).wait_recv()

    def arrive_chip(s, late):
        both = tiles.at[chip_here, s, pl.ds(2 * late, 2)]
        remote(both, both, sent.at[3], chip_recv.at[s, late], chip_dev).wait_recv()

    def row_stats(dt, dh):
        a = 1 - dt
        s = jnp.where(odd == (dh + 1) // 2, 2, 1) * dh * dh
        return remote(stats.at[1, 0], stats.at[a, s], stats_send.at[a, dh + 1], stats_recv.at[a, s], (t + dt, h + dh))

    def spread(s, k):
        @pl.when(~(relay | bound) if s == 2 and k not in DIRECT else ~relay)
        def _():
            off_chip(s, k).start()

        to_chip(s, k).start()

    def begin(k):
        swap(k).start()

        @pl.when(~relay)
        def _():
            off_chip(0, k).start()

    def on_swap(k):
        swap(k).wait_recv()

        @pl.when(z_to)
        def _():
            along_z(k).start()

        spread(1, k)

    def on_z(k):
        @pl.when(z_from)
        def _():
            along_z(k).wait_recv()
            spread(2, k)

    def on_relay(k):
        arrive(0, k)
        off_chip(0, k).start()

    def on_side(k):
        arrive(1, k)

        @pl.when(z_to)
        def _():
            side_z(k).start()

    for copy in copies:
        copy.wait()
    for k in range(CHUNKS):
        if k in range(6):
            begin(k)
        to_chip(0, k).start()

    clip = clip_ref[0]

    def columns(n):
        return slice(n * dim, (n + 1) * dim)

    row_max[...] = jnp.full(row_max.shape, NEGATIVE, jnp.float32)
    for ref in (acc, grad, row_sum, row_dot, key_acc, value_acc):
        ref[...] = jnp.zeros(ref.shape, ref.dtype)
    stats[1, 0] = jnp.zeros(stats.shape[2:], jnp.float32)
    for n in range(HEADS):
        out_grad_t[n] = tiles[1, 0, G, :, columns(n)].astype(jnp.float32).T

    EVENTS = (
        {
            0: [(on_swap, 0)],
            1: [(on_swap, 1)],
            2: [(on_swap, 2), (on_z, 0), (on_swap, 3)],
            3: [(on_swap, 4), (on_z, 1), (on_swap, 5), (begin, 6), (begin, 7), (on_z, 2), (begin, 8)],
            4: [(on_z, 3)],
            5: [(on_z, 4), (on_swap, 6)],
            6: [(on_z, 5), (on_swap, 7), (begin, 9), (begin, 10), (begin, 11)],
            7: [(on_swap, 8), (on_z, 6)],
            8: [(on_z, 7), (on_swap, 9)],
            9: [(on_swap, 10)],
            10: [(on_swap, 11), (on_z, 8)],
            11: [(on_z, 9), (on_z, 10)],
            12: [(on_z, 11)],
        },
        {
            2: [(on_swap, 0), (on_swap, 1), (on_swap, 2), (on_z, 0), (on_swap, 3), (on_z, 1), (on_swap, 4), (on_swap, 5)],
            3: [(on_z, 2), (on_side, 0), (on_z, 3), (on_side, 1)],
            4: [(begin, 6), (begin, 7), (begin, 8), (on_side, 2), (on_z, 4), (on_side, 3), (on_z, 5)],
            5: [(on_side, 4)],
            6: [(on_side, 5), (begin, 9), (begin, 10), (on_swap, 6), (begin, 11)],
            7: [(on_swap, 7)],
            8: [(on_swap, 8)],
            9: [(on_swap, 9), (on_z, 6)],
            10: [(on_swap, 10), (on_z, 7), (on_swap, 11), (on_z, 8)],
            11: [(on_side, 6), (on_z, 9), (on_side, 7), (on_side, 8), (on_z, 10)],
            12: [(on_z, 11)],
        },
        {
            2: [(on_relay, 0), (on_relay, 1), (on_swap, 0), (on_relay, 2), (on_relay, 3), (on_swap, 1), (on_relay, 4), (on_relay, 5), (on_swap, 2), (on_z, 0), (on_swap, 3), (on_z, 1), (on_swap, 4), (on_swap, 5), (on_z, 2)],
            3: [(begin, 6), (begin, 7), (on_z, 3), (on_z, 4), (on_z, 5)],
            4: [(begin, 8)],
            5: [(begin, 9), (begin, 10), (begin, 11), (on_relay, 6), (on_relay, 7), (on_relay, 8), (on_swap, 6)],
            6: [(on_swap, 7), (on_swap, 8)],
            7: [(on_relay, 9), (on_swap, 9), (on_relay, 10), (on_relay, 11), (on_z, 6), (on_swap, 10)],
            8: [(on_z, 7), (on_swap, 11), (on_z, 8), (on_z, 9), (on_z, 10)],
            9: [(on_z, 11)],
        },
    )
    WORDS = (
        (172065856, 422879462, 761878004),
        (73534496, 691314855, 761877996),
        (241306656, 761975401, 762010326),
    )
    STEPS = 17

    kinds = (~(relay | bound), bound, relay)

    def events_at(step):
        for mine, events in zip(kinds, EVENTS):
            if step in events:
                @pl.when(mine)
                def _():
                    for entry in events[step]:
                        entry[0](*entry[1:])

    def dispatch(step, low, high):
        if high - low == 1:
            events_at(low)
        elif high > low:
            middle = (low + high) // 2

            @pl.when(step < middle)
            def _():
                dispatch(step, low, middle)

            @pl.when(step >= middle)
            def _():
                dispatch(step, middle, high)

    def word(i):
        return jnp.where(relay, WORDS[2][i], jnp.where(bound, WORDS[1][i], WORDS[0][i]))

    def queries_side(a, s, related):
        heads = range(HEADS)
        key = [tiles[a, s, K, :, columns(n)] for n in heads]
        value = [tiles[a, s, V, :, columns(n)] for n in heads]
        scores = [nt(key[n], tiles[1, 0, Q, :, columns(n)]) for n in heads]
        grad_weights = [nt(value[n], tiles[1, 0, G, :, columns(n)]) for n in heads]
        key_t = [key[n].T for n in heads]
        both_t = [jnp.concatenate([value[n].T, key_t[n]], axis=0) for n in heads]
        fades, raised, totals, dots = [], [], [], []
        for n in heads:
            top = jnp.where(related, jnp.max(scores[n], axis=0, keepdims=True) * to_log2, NEGATIVE)
            old_max = row_max[n]
            new_max = jnp.maximum(old_max, top)
            fades.append(jnp.exp2(old_max - new_max))
            raised.append(jnp.exp2(scores[n] * to_log2 - jnp.where(related, new_max, -NEGATIVE)))
            totals.append(row_sum[n] * fades[n] + jnp.sum(raised[n], axis=0, keepdims=True))
            row_max[n] = new_max
            row_sum[n] = totals[n]
        for n in heads:
            old = acc[n]
            new = old * fades[n] + nn(both_t[n], raised[n].astype(jnp.bfloat16))
            dots.append(jnp.sum(out_grad_t[n] * new[:dim], axis=0, keepdims=True) / totals[n])
            grad[n] = (grad[n] - (dots[n] - row_dot[n]) * old[dim:]) * fades[n]
            acc[n] = new
            row_dot[n] = dots[n]
        for n in heads:
            inner = (raised[n] * (grad_weights[n] - dots[n])).astype(jnp.bfloat16)
            grad[n] += nn(key_t[n], inner)

    def finish_queries():
        finish = []
        for n in range(HEADS):
            total = row_sum[n]
            sums = acc[n]
            attended = (sums[:dim] / total).astype(jnp.bfloat16).astype(jnp.float32)
            dot = jnp.sum(out_grad_t[n] * attended, axis=0, keepdims=True)
            stats[1, 0, n : n + 1] = row_max[n] + jnp.log2(total)
            stats[1, 0, HEADS + n : HEADS + n + 1] = dot
            finish.append((dot, total, sums, attended))
        for dt, dh in neighbours:
            @pl.when(exists(dt, dh))
            def _():
                row_stats(dt, dh).start()

        for n in range(HEADS):
            dot, total, sums, attended = finish[n]
            out_ref[0, :, columns(n)] = attended.T.astype(jnp.bfloat16)
            own_grad = (grad[n] - (dot - row_dot[n]) * sums[dim:]) * (scale / total)
            out_ref[1, :, columns(n)] = own_grad.T.astype(jnp.bfloat16)

    def keys_side(s, frames):
        for n in range(HEADS):
            own_k, own_v = tiles[1, 0, K, :, columns(n)], tiles[1, 0, V, :, columns(n)]
            to_value, to_key = [], []
            for a, counts in frames:
                query, out_grad = tiles[a, s, Q, :, columns(n)], tiles[a, s, G, :, columns(n)]
                log_total = jnp.where(counts, stats[a, s, n : n + 1], -NEGATIVE)
                dot = stats[a, s, HEADS + n : HEADS + n + 1]
                weights = jnp.exp2(nt(own_k, query) * to_log2 - log_total)
                inner = (weights * (nt(own_v, out_grad) - dot)).astype(jnp.bfloat16)
                to_value.append(nn(weights.astype(jnp.bfloat16), out_grad))
                to_key.append(nn(inner, query))
            value_acc[n] += sum(to_value[1:], to_value[0])
            key_acc[n] += sum(to_key[1:], to_key[0])

    def frame(o):
        a = jnp.where(o == 0, 1, jnp.where(o == 1, chip_here, off_here))
        return a, ((t + a - 1) >= clip) == (t >= clip)

    def arrive_stats(a, s):
        remote(stats.at[1, 0], stats.at[a, s], stats_send.at[1, 1], stats_recv.at[a, s], chip_dev).wait_recv()

    def do_step(step, left_words):
        dispatch(step, 0, STEPS)
        now, later = left_words[0], left_words[1:]
        digit = now % 32
        s, o = digit // 3, digit % 3

        @pl.when((digit < 9) & ((s < 2) | z_from) & ((o < 2) | ~relay))
        def _():
            @pl.when(o == 1)
            def _():
                arrive_chip(s, 0)

            @pl.when((o == 2) & ~(bound & (s == 1)))
            def _():
                for k in range(EARLY):
                    arrive(s, k)

            queries_side(frame(o)[0], s, frame(o)[1])

        @pl.when(digit == FINISH)
        def _():
            finish_queries()

        single = digit - KEYS
        row, o = single // 3, single % 3

        @pl.when((digit >= KEYS) & (digit < PAIRS) & ((row < 2) | z_from) & ((o < 2) | ~relay))
        def _():
            @pl.when(o == 1)
            def _():
                arrive_chip(row, 1)

            @pl.when(o == 2)
            def _():
                for k in range(EARLY, CHUNKS):
                    if k in DIRECT:
                        arrive(row, k)
                    else:
                        @pl.when(~(bound & (row == 1)))
                        def _():
                            arrive(row, k)

            @pl.when(single > 0)
            def _():
                arrive_stats(frame(o)[0], row)

            keys_side(row, (frame(o),))

        pair = digit - PAIRS

        @pl.when((digit >= PAIRS) & (digit < NOTHING) & ((pair < 2) | z_from))
        def _():
            arrive_chip(pair, 1)
            arrive_stats(chip_here, pair)

            @pl.when(pair > 0)
            def _():
                arrive_stats(1, pair)

            keys_side(pair, (frame(0), frame(1)))

        turn = step % 6 == 5
        return tuple(
            jnp.where(turn, after, before) for before, after in zip((now // 32,) + later, later + (jnp.int32(0),))
        )

    lax.fori_loop(0, STEPS, do_step, tuple(word(i) for i in range(len(WORDS[0]))))

    for n in range(HEADS):
        out_ref[2, :, columns(n)] = (key_acc[n] * scale).astype(jnp.bfloat16)
        out_ref[3, :, columns(n)] = value_acc[n].astype(jnp.bfloat16)

    def drain(place, arrays=4):
        whole = tiles.at[1, 0, pl.ds(0, arrays)]
        remote(whole, whole, sent.at[place], sent.at[place], chip_dev).wait_send()

    direct = len(DIRECT) // PIECES
    usual = ~(relay | bound)
    for place in (0, 3, 4, 6):
        drain(place)
    for place, used, arrays in (
        (1, z_to, 4), (2, z_to & bound, 4 - direct), (5, z_from, 4), (7, ~relay, 4), (8, z_from & usual, 4), (8, z_from & bound, direct)
    ):
        if arrays:
            @pl.when(used)
            def _():
                drain(place, arrays)

    for dt, dh in neighbours:
        @pl.when(exists(dt, dh))
        def _():
            row_stats(dt, dh).wait_send()


def shards(queries, key_states, value_states, out_grad, clip_start):
    rows, channels = queries.shape[-2:]
    dim = channels // HEADS
    flat = [
        pltpu.with_memory_space_constraint(x.reshape(rows, channels), pltpu.HBM)
        for x in (queries, key_states, value_states, out_grad)
    ]
    vmem = pl.BlockSpec(memory_space=pltpu.VMEM)
    outs = pl.pallas_call(
        kernel,
        out_shape=pltpu.VMEM((4, rows, channels), jnp.bfloat16),
        in_specs=[pl.BlockSpec(memory_space=pltpu.SMEM)] + [pl.BlockSpec(memory_space=pltpu.HBM)] * 4,
        out_specs=vmem,
        scratch_shapes=[
            pltpu.VMEM((3, 3, 4, rows, channels), jnp.bfloat16),
            pltpu.VMEM((3, 3, 8, rows), jnp.float32),
            pltpu.VMEM((HEADS, dim, rows), jnp.float32),
            pltpu.VMEM((HEADS, 2 * dim, rows), jnp.float32),
            pltpu.VMEM((HEADS, dim, rows), jnp.float32),
            pltpu.VMEM((HEADS, 1, rows), jnp.float32),
            pltpu.VMEM((HEADS, 1, rows), jnp.float32),
            pltpu.VMEM((HEADS, 1, rows), jnp.float32),
            pltpu.VMEM((HEADS, rows, dim), jnp.float32),
            pltpu.VMEM((HEADS, rows, dim), jnp.float32),
            pltpu.SemaphoreType.DMA((4,)),
            pltpu.SemaphoreType.DMA((9,)),
            pltpu.SemaphoreType.DMA((CHUNKS,)),
            pltpu.SemaphoreType.DMA((CHUNKS,)),
            pltpu.SemaphoreType.DMA((3, 2)),
            pltpu.SemaphoreType.DMA((3, CHUNKS)),
            pltpu.SemaphoreType.DMA((3, 3)),
            pltpu.SemaphoreType.DMA((3, 3)),
        ],
        compiler_params=pltpu.CompilerParams(
            collective_id=0, has_side_effects=True, vmem_limit_bytes=48 * 2**20
        ),
        name="tile_attention",
    )(clip_start, *flat)
    return tuple(outs[i].reshape(queries.shape) for i in range(4))


def solution(mesh):
    spec = P("tm", "height", None, None, None)
    return jax.shard_map(
        shards, mesh=mesh, in_specs=(spec,) * 4 + (P(),), out_specs=(spec,) * 4, check_vma=False
    )
```

```python
import jax
import jax.numpy as jnp
from jax import lax
from jax.experimental import pallas as pl
from jax.experimental.pallas import tpu as pltpu
from jax.sharding import PartitionSpec as P

HEADS = 2
LOG2E = 1.4426950408889634
NEGATIVE = -1e30
MESH = pl.DeviceIdType.MESH
FINISH, KEYS, PAIRS, NOTHING = 9, 10, 19, 22
K, V, Q, G = range(4)
PIECES = 3
EARLY = 2 * PIECES
CHUNKS = 4 * PIECES
DIRECT = (9, 10, 11,)


def nt(left, right):
    return lax.dot_general(left, right, (((1,), (1,)), ((), ())), preferred_element_type=jnp.float32)


def nn(left, right):
    return jnp.dot(left, right, preferred_element_type=jnp.float32)


def kernel(
    clip_ref, q_in, k_in, v_in, g_in, out_ref,
    tiles, stats, out_grad_t, acc, grad, row_max, row_sum, row_dot, key_acc, value_acc,
    local_sem, sent, swap_recv, z_recv, chip_recv, off_recv, stats_send, stats_recv,
):
    t = lax.axis_index("tm")
    h = lax.axis_index("height")
    core, odd, z = t % 2, h % 2, h // 2
    dim = q_in.shape[-1] // HEADS
    scale = dim ** (-0.5)
    to_log2 = scale * LOG2E

    copies = [pltpu.make_async_copy(ref, tiles.at[1, 0, u], local_sem.at[u]) for u, ref in enumerate((k_in, v_in, q_in, g_in))]
    for copy in copies:
        copy.start()

    first, last, left, right = t == 0, t == 15, t == 7, t == 8
    relay, bound = first | last, left | right
    other = h + 1 - 2 * odd
    chip_dev = (t + 1 - 2 * core, h)
    z_to = jnp.where(odd == 0, z < 3, z > 0)
    z_from = jnp.where(odd == 0, z > 0, z < 3)
    z_dst = (t, h + 2 - 4 * odd)
    z_src = (t, h - 2 + 4 * odd)
    chip_there = jnp.where(core == 0, 0, 2)
    chip_here = 2 - chip_there
    off_here = chip_there
    near = jnp.where(core == 1, t + 1, t - 1)
    near_slot = jnp.where(core == 1, 0, 2)

    def pick(at_left, at_right, at_last, at_first, usual):
        return jnp.where(left, at_left, jnp.where(right, at_right, jnp.where(last, at_last, jnp.where(first, at_first, usual))))

    own_dev, own_slot = pick(0, 15, 7, 8, near), pick(0, 2, 2, 0, near_slot)
    off_from = pick(1, 1, 2, 0, 1)

    neighbours = [(dt, dh) for dt in (-1, 0, 1) for dh in (-1, 0, 1) if dt or dh]

    def exists(dt, dh):
        return (t + dt >= 0) & (t + dt <= 15) & (h + dh >= 0) & (h + dh <= 7)

    barrier = pltpu.get_barrier_semaphore()

    def greet(frame, row):
        pl.semaphore_signal(barrier, inc=1, device_id=(frame, row), device_id_type=MESH)

    targets = (relay | bound).astype(jnp.int32) + z_to.astype(jnp.int32)
    for dt, dh in neighbours:
        targets = targets + exists(dt, dh).astype(jnp.int32)

        @pl.when(exists(dt, dh))
        def _():
            greet(t + dt, h + dh)

    @pl.when(relay | bound)
    def _():
        greet(pick(15, 0, 8, 7, 0), h)

    @pl.when(z_from)
    def _():
        greet(*z_src)

    pl.semaphore_wait(barrier, targets)

    def part(a, s, k):
        u, piece = k // PIECES, k % PIECES
        size = tiles.shape[3] // PIECES
        return tiles.at[a, s, u, pl.ds(piece * size, size)]

    def remote(src, dst, send, recv, device):
        return pltpu.make_async_remote_copy(
            src_ref=src, dst_ref=dst, send_sem=send, recv_sem=recv, device_id=device, device_id_type=MESH
        )

    def swap(k):
        return remote(part(1, 0, k), part(1, 1, k), sent.at[0], swap_recv.at[k], (t, other))

    def along_z(k):
        return remote(part(1, 1, k), part(1, 2, k), sent.at[1], z_recv.at[k], z_dst)

    def side_z(k):
        return remote(part(off_here, 1, k), part(off_here, 2, k), sent.at[2], off_recv.at[2, k], z_dst)

    def to_chip(s, k):
        return remote(part(1, s, k), part(chip_there, s, k), sent.at[3 + s], chip_recv.at[s, k // EARLY], chip_dev)

    def off_chip(s, k):
        frame, slot = (near, near_slot) if s else (own_dev, own_slot)
        return remote(part(off_from, s, k), part(slot, s, k), sent.at[6 + s], off_recv.at[s, k], (frame, h))

    def arrive(s, k):
        remote(part(1, s, k), part(off_here, s, k), sent.at[6], off_recv.at[s, k], chip_dev).wait_recv()

    def arrive_chip(s, late):
        both = tiles.at[chip_here, s, pl.ds(2 * late, 2)]
        remote(both, both, sent.at[3], chip_recv.at[s, late], chip_dev).wait_recv()

    def row_stats(dt, dh):
        a = 1 - dt
        s = jnp.where(odd == (dh + 1) // 2, 2, 1) * dh * dh
        return remote(stats.at[1, 0], stats.at[a, s], stats_send.at[a, dh + 1], stats_recv.at[a, s], (t + dt, h + dh))

    def spread(s, k):
        @pl.when(~(relay | bound) if s == 2 and k not in DIRECT else ~relay)
        def _():
            off_chip(s, k).start()

        to_chip(s, k).start()

    def begin(k):
        swap(k).start()

        @pl.when(~relay)
        def _():
            off_chip(0, k).start()

    def on_swap(k):
        swap(k).wait_recv()

        @pl.when(z_to)
        def _():
            along_z(k).start()

        spread(1, k)

    def on_z(k):
        @pl.when(z_from)
        def _():
            along_z(k).wait_recv()
            spread(2, k)

    def on_relay(k):
        arrive(0, k)
        off_chip(0, k).start()

    def on_side(k):
        arrive(1, k)

        @pl.when(z_to)
        def _():
            side_z(k).start()

    for copy in copies:
        copy.wait()
    for k in range(CHUNKS):
        if k in range(6):
            begin(k)
        to_chip(0, k).start()

    clip = clip_ref[0]

    def columns(n):
        return slice(n * dim, (n + 1) * dim)

    row_max[...] = jnp.full(row_max.shape, NEGATIVE, jnp.float32)
    for ref in (acc, grad, row_sum, row_dot, key_acc, value_acc):
        ref[...] = jnp.zeros(ref.shape, ref.dtype)
    stats[1, 0] = jnp.zeros(stats.shape[2:], jnp.float32)
    for n in range(HEADS):
        out_grad_t[n] = tiles[1, 0, G, :, columns(n)].astype(jnp.float32).T

    EVENTS = (
        {
            2: [(on_swap, 0), (on_swap, 1)],
            3: [(on_swap, 2), (on_z, 0), (on_swap, 3), (on_z, 1), (on_swap, 4), (on_swap, 5), (on_z, 2), (begin, 6), (begin, 7), (begin, 8)],
            4: [(on_z, 3)],
            5: [(on_z, 4), (on_swap, 6)],
            6: [(on_z, 5), (on_swap, 7), (begin, 9), (begin, 10), (begin, 11)],
            7: [(on_swap, 8), (on_z, 6)],
            8: [(on_z, 7), (on_swap, 9)],
            9: [(on_swap, 10)],
            10: [(on_z, 8), (on_swap, 11), (on_z, 9)],
            11: [(on_z, 10)],
            12: [(on_z, 11)],
        },
        {
            1: [(on_swap, 0), (on_swap, 1), (on_swap, 2)],
            2: [(on_z, 0), (on_swap, 3), (on_z, 1), (on_swap, 4), (on_swap, 5)],
            3: [(on_z, 2), (on_side, 0), (on_z, 3), (on_side, 1)],
            4: [(begin, 6), (begin, 7), (on_side, 2), (on_side, 3), (begin, 8), (on_z, 4), (on_z, 5)],
            5: [(on_side, 4)],
            6: [(on_side, 5), (begin, 9), (begin, 10), (on_swap, 6), (begin, 11)],
            7: [(on_swap, 7)],
            8: [(on_swap, 8)],
            9: [(on_swap, 9), (on_z, 6)],
            10: [(on_swap, 10), (on_z, 7), (on_z, 8), (on_swap, 11)],
            11: [(on_side, 6), (on_z, 9), (on_side, 7), (on_side, 8), (on_z, 10)],
            12: [(on_z, 11)],
        },
        {
            2: [(on_relay, 0), (on_relay, 1), (on_swap, 0), (on_relay, 2), (on_relay, 3), (on_swap, 1), (on_relay, 4), (on_relay, 5), (on_swap, 2), (on_z, 0), (on_swap, 3), (on_z, 1), (on_z, 2), (on_swap, 4), (on_swap, 5)],
            3: [(begin, 6), (begin, 7), (on_z, 3), (begin, 8)],
            4: [(on_z, 4), (on_z, 5)],
            5: [(begin, 9), (begin, 10), (begin, 11), (on_relay, 6), (on_relay, 7), (on_relay, 8), (on_swap, 6)],
            6: [(on_swap, 7)],
            7: [(on_swap, 8), (on_relay, 9), (on_swap, 9), (on_relay, 10), (on_relay, 11), (on_z, 6), (on_swap, 10)],
            8: [(on_z, 7), (on_swap, 11), (on_z, 8), (on_z, 9), (on_z, 10)],
            9: [(on_z, 11)],
        },
    )
    WORDS = (
        (172066848, 422879462, 761878004),
        (73534496, 691314855, 761872044),
        (241306656, 761975401, 762010326),
    )
    STEPS = 17

    kinds = (~(relay | bound), bound, relay)

    def events_at(step):
        for mine, events in zip(kinds, EVENTS):
            if step in events:
                @pl.when(mine)
                def _():
                    for entry in events[step]:
                        entry[0](*entry[1:])

    def dispatch(step, low, high):
        if high - low == 1:
            events_at(low)
        elif high > low:
            middle = (low + high) // 2

            @pl.when(step < middle)
            def _():
                dispatch(step, low, middle)

            @pl.when(step >= middle)
            def _():
                dispatch(step, middle, high)

    def word(i):
        return jnp.where(relay, WORDS[2][i], jnp.where(bound, WORDS[1][i], WORDS[0][i]))

    def queries_side(a, s, related):
        heads = range(HEADS)
        key = [tiles[a, s, K, :, columns(n)] for n in heads]
        value = [tiles[a, s, V, :, columns(n)] for n in heads]
        scores = [nt(key[n], tiles[1, 0, Q, :, columns(n)]) for n in heads]
        grad_weights = [nt(value[n], tiles[1, 0, G, :, columns(n)]) for n in heads]
        key_t = [key[n].T for n in heads]
        both_t = [jnp.concatenate([value[n].T, key_t[n]], axis=0) for n in heads]
        fades, raised, totals, dots = [], [], [], []
        for n in heads:
            top = jnp.where(related, jnp.max(scores[n], axis=0, keepdims=True) * to_log2, NEGATIVE)
            old_max = row_max[n]
            new_max = jnp.maximum(old_max, top)
            fades.append(jnp.exp2(old_max - new_max))
            raised.append(jnp.exp2(scores[n] * to_log2 - jnp.where(related, new_max, -NEGATIVE)))
            totals.append(row_sum[n] * fades[n] + jnp.sum(raised[n], axis=0, keepdims=True))
            row_max[n] = new_max
            row_sum[n] = totals[n]
        for n in heads:
            old = acc[n]
            new = old * fades[n] + nn(both_t[n], raised[n].astype(jnp.bfloat16))
            dots.append(jnp.sum(out_grad_t[n] * new[:dim], axis=0, keepdims=True) / totals[n])
            grad[n] = (grad[n] - (dots[n] - row_dot[n]) * old[dim:]) * fades[n]
            acc[n] = new
            row_dot[n] = dots[n]
        for n in heads:
            inner = (raised[n] * (grad_weights[n] - dots[n])).astype(jnp.bfloat16)
            grad[n] += nn(key_t[n], inner)

    def finish_queries():
        finish = []
        for n in range(HEADS):
            total = row_sum[n]
            sums = acc[n]
            attended = (sums[:dim] / total).astype(jnp.bfloat16).astype(jnp.float32)
            dot = jnp.sum(out_grad_t[n] * attended, axis=0, keepdims=True)
            stats[1, 0, n : n + 1] = row_max[n] + jnp.log2(total)
            stats[1, 0, HEADS + n : HEADS + n + 1] = dot
            finish.append((dot, total, sums, attended))
        for dt, dh in neighbours:
            @pl.when(exists(dt, dh))
            def _():
                row_stats(dt, dh).start()

        for n in range(HEADS):
            dot, total, sums, attended = finish[n]
            out_ref[0, :, columns(n)] = attended.T.astype(jnp.bfloat16)
            own_grad = (grad[n] - (dot - row_dot[n]) * sums[dim:]) * (scale / total)
            out_ref[1, :, columns(n)] = own_grad.T.astype(jnp.bfloat16)

    def keys_side(s, frames):
        for n in range(HEADS):
            own_k, own_v = tiles[1, 0, K, :, columns(n)], tiles[1, 0, V, :, columns(n)]
            to_value, to_key = [], []
            for a, counts in frames:
                query, out_grad = tiles[a, s, Q, :, columns(n)], tiles[a, s, G, :, columns(n)]
                log_total = jnp.where(counts, stats[a, s, n : n + 1], -NEGATIVE)
                dot = stats[a, s, HEADS + n : HEADS + n + 1]
                weights = jnp.exp2(nt(own_k, query) * to_log2 - log_total)
                inner = (weights * (nt(own_v, out_grad) - dot)).astype(jnp.bfloat16)
                to_value.append(nn(weights.astype(jnp.bfloat16), out_grad))
                to_key.append(nn(inner, query))
            value_acc[n] += sum(to_value[1:], to_value[0])
            key_acc[n] += sum(to_key[1:], to_key[0])

    def frame(o):
        a = jnp.where(o == 0, 1, jnp.where(o == 1, chip_here, off_here))
        return a, ((t + a - 1) >= clip) == (t >= clip)

    def arrive_stats(a, s):
        remote(stats.at[1, 0], stats.at[a, s], stats_send.at[1, 1], stats_recv.at[a, s], chip_dev).wait_recv()

    def do_step(step, left_words):
        dispatch(step, 0, STEPS)
        now, later = left_words[0], left_words[1:]
        digit = now % 32
        s, o = digit // 3, digit % 3

        @pl.when((digit < 9) & ((s < 2) | z_from) & ((o < 2) | ~relay))
        def _():
            @pl.when(o == 1)
            def _():
                arrive_chip(s, 0)

            @pl.when((o == 2) & ~(bound & (s == 1)))
            def _():
                for k in range(EARLY):
                    arrive(s, k)

            queries_side(frame(o)[0], s, frame(o)[1])

        @pl.when(digit == FINISH)
        def _():
            finish_queries()

        single = digit - KEYS
        row, o = single // 3, single % 3

        @pl.when((digit >= KEYS) & (digit < PAIRS) & ((row < 2) | z_from) & ((o < 2) | ~relay))
        def _():
            @pl.when(o == 1)
            def _():
                arrive_chip(row, 1)

            @pl.when(o == 2)
            def _():
                for k in range(EARLY, CHUNKS):
                    if k in DIRECT:
                        arrive(row, k)
                    else:
                        @pl.when(~(bound & (row == 1)))
                        def _():
                            arrive(row, k)

            @pl.when(single > 0)
            def _():
                arrive_stats(frame(o)[0], row)

            keys_side(row, (frame(o),))

        pair = digit - PAIRS

        @pl.when((digit >= PAIRS) & (digit < NOTHING) & ((pair < 2) | z_from))
        def _():
            arrive_chip(pair, 1)
            arrive_stats(chip_here, pair)

            @pl.when(pair > 0)
            def _():
                arrive_stats(1, pair)

            keys_side(pair, (frame(0), frame(1)))

        turn = step % 6 == 5
        return tuple(
            jnp.where(turn, after, before) for before, after in zip((now // 32,) + later, later + (jnp.int32(0),))
        )

    lax.fori_loop(0, STEPS, do_step, tuple(word(i) for i in range(len(WORDS[0]))))

    for n in range(HEADS):
        out_ref[2, :, columns(n)] = (key_acc[n] * scale).astype(jnp.bfloat16)
        out_ref[3, :, columns(n)] = value_acc[n].astype(jnp.bfloat16)

    def drain(place, arrays=4):
        whole = tiles.at[1, 0, pl.ds(0, arrays)]
        remote(whole, whole, sent.at[place], sent.at[place], chip_dev).wait_send()

    direct = len(DIRECT) // PIECES
    usual = ~(relay | bound)
    for place in (0, 3, 4, 6):
        drain(place)
    for place, used, arrays in (
        (1, z_to, 4), (2, z_to & bound, 4 - direct), (5, z_from, 4), (7, ~relay, 4), (8, z_from & usual, 4), (8, z_from & bound, direct)
    ):
        if arrays:
            @pl.when(used)
            def _():
                drain(place, arrays)

    for dt, dh in neighbours:
        @pl.when(exists(dt, dh))
        def _():
            row_stats(dt, dh).wait_send()


def shards(queries, key_states, value_states, out_grad, clip_start):
    rows, channels = queries.shape[-2:]
    dim = channels // HEADS
    flat = [
        pltpu.with_memory_space_constraint(x.reshape(rows, channels), pltpu.HBM)
        for x in (queries, key_states, value_states, out_grad)
    ]
    vmem = pl.BlockSpec(memory_space=pltpu.VMEM)
    outs = pl.pallas_call(
        kernel,
        out_shape=pltpu.VMEM((4, rows, channels), jnp.bfloat16),
        in_specs=[pl.BlockSpec(memory_space=pltpu.SMEM)] + [pl.BlockSpec(memory_space=pltpu.HBM)] * 4,
        out_specs=vmem,
        scratch_shapes=[
            pltpu.VMEM((3, 3, 4, rows, channels), jnp.bfloat16),
            pltpu.VMEM((3, 3, 8, rows), jnp.float32),
            pltpu.VMEM((HEADS, dim, rows), jnp.float32),
            pltpu.VMEM((HEADS, 2 * dim, rows), jnp.float32),
            pltpu.VMEM((HEADS, dim, rows), jnp.float32),
            pltpu.VMEM((HEADS, 1, rows), jnp.float32),
            pltpu.VMEM((HEADS, 1, rows), jnp.float32),
            pltpu.VMEM((HEADS, 1, rows), jnp.float32),
            pltpu.VMEM((HEADS, rows, dim), jnp.float32),
            pltpu.VMEM((HEADS, rows, dim), jnp.float32),
            pltpu.SemaphoreType.DMA((4,)),
            pltpu.SemaphoreType.DMA((9,)),
            pltpu.SemaphoreType.DMA((CHUNKS,)),
            pltpu.SemaphoreType.DMA((CHUNKS,)),
            pltpu.SemaphoreType.DMA((3, 2)),
            pltpu.SemaphoreType.DMA((3, CHUNKS)),
            pltpu.SemaphoreType.DMA((3, 3)),
            pltpu.SemaphoreType.DMA((3, 3)),
        ],
        compiler_params=pltpu.CompilerParams(
            collective_id=0, has_side_effects=True, vmem_limit_bytes=48 * 2**20
        ),
        name="tile_attention",
    )(clip_start, *flat)
    return tuple(outs[i].reshape(queries.shape) for i in range(4))


def solution(mesh):
    spec = P("tm", "height", None, None, None)
    return jax.shard_map(
        shards, mesh=mesh, in_specs=(spec,) * 4 + (P(),), out_specs=(spec,) * 4, check_vma=False
    )
```
